32 devices in a mesh: blk: 4 (over y, x), inner: 8 (over z, core).
Axes of the slice: x: 2, y: 2, z: 4, core: 2. Of those that a mesh axis runs over, the one named last changes fastest.
Arguments:
- queries: bfloat16 [4096, 768], P(('blk', 'inner')), may hold values from -16 to 16
- keys: bfloat16 [4096, 768], P(('blk', 'inner')), may hold values from -16 to 16
- values: bfloat16 [4096, 768], P(('blk', 'inner')), may hold values from -6 to 6
- valid: int32 [4096], P(('blk', 'inner')), may hold values 0 or 1
- out_weight: bfloat16 [768, 768], replicated, may hold values from -0.21875 to 0.21875
Outputs:
- mixed: bfloat16 [4096, 768], P(('blk', 'inner'))
The draws below stay inside these ranges and needn't reach their ends.
All inputs are finite; a program needn't handle non-finite values. No bound on the sum of `valid` on one device may be relied on, other than what follows from the above.
Results may differ from the reference program's by a relative error of at most 0.015.
Values may be sent and summed in bfloat16 or wider, within the bound.
No kernel may reach another device: no remote copies, remote signals or barrier semaphores. Data moves between devices by JAX's collectives and lax.ppermute only.
A program may use at most 128 MiB of HBM per device.

```python
import jax
import jax.numpy as jnp
from jax import lax

HEADS = 12
HEAD_DIM = 64
D = 768
TOKENS = 4096


def draw_queries(key, part):
    subkey = jax.random.fold_in(key, 1)
    drawn = jnp.clip(jax.random.normal(subkey, (TOKENS, D), jnp.float32), -8.0, 8.0)
    return drawn.astype(jnp.bfloat16)


def draw_keys(key, part):
    subkey = jax.random.fold_in(key, 2)
    drawn = jnp.clip(jax.random.normal(subkey, (TOKENS, D), jnp.float32), -8.0, 8.0)
    return drawn.astype(jnp.bfloat16)


def place_ends(values, own_key, least, top_value):
    shape = values.shape
    index_at = [jax.random.randint(jax.random.fold_in(own_key, axis), (), 0, shape[axis]) for axis in range(len(shape))]
    values = values.at[tuple(index_at)].set(least)
    longest = shape.index(max(shape))
    index_at[longest] = (index_at[longest] + 1) % shape[longest]
    return values.at[tuple(index_at)].set(top_value)


def levels(key, extent, pieces, least, high):
    def one(dim, parts):
        draws = jax.random.uniform(jax.random.fold_in(jax.random.fold_in(key, 6), dim), (parts,), jnp.float32, least / len(pieces), high / len(pieces))
        return jnp.repeat(jnp.exp(draws), extent[dim] // parts).reshape((-1,) + (1,) * (len(extent) - dim - 1))

    loudness = one(*pieces[0])
    for cut in pieces[1:]:
        loudness = loudness * one(*cut)
    return loudness


def centred(stream_key, extent, spread, most, pieces=(), kind=jnp.bfloat16):
    values = spread * jax.random.normal(stream_key, extent, jnp.float32)
    if pieces:
        values = values * levels(stream_key, extent, pieces, -0.22, 0.18)
    return jnp.clip(values, -most, most).astype(kind)


def setup_inputs(seed: int = 0) -> dict:
    seeds = jax.random.split(jax.random.key(seed), 6)
    queries = draw_queries(jax.random.fold_in(seeds[5], 71), 0)
    keys = draw_keys(jax.random.fold_in(seeds[5], 71), 0)
    values = centred(seeds[2], (TOKENS, D), 1.0, 6.0, ((0, 32),))
    valid = place_ends((jax.random.randint(seeds[3], (TOKENS,), 0, 4) < 3).astype(jnp.int32), jax.random.fold_in(seeds[3], 1), 0, 1)
    out_weight = centred(seeds[4], (D, D), D ** -0.5, 0.21875)
    return dict(queries=queries, keys=keys, values=values, valid=valid, out_weight=out_weight)


def reference(queries, keys, values, valid, out_weight):
    score_scale = HEAD_DIM ** -0.5
    key_heads = keys.astype(jnp.float32).reshape(TOKENS, HEADS, HEAD_DIM)
    value_heads = values.astype(jnp.float32).reshape(TOKENS, HEADS, HEAD_DIM)
    usable = valid > 0
    block_rows = min(512, TOKENS)

    def attend_block(query_block):
        query_heads = query_block.astype(jnp.float32).reshape(block_rows, HEADS, HEAD_DIM)
        scores = jnp.einsum("qhd,khd->hqk", query_heads, key_heads) * score_scale
        scores = jnp.where(usable[None, None, :], scores, -1e30)
        row_top = jnp.maximum(jnp.max(scores, axis=-1), 0.0)
        chances = jnp.exp(scores - row_top[..., None]).astype(jnp.bfloat16)
        chances = lax.optimization_barrier(chances).astype(jnp.float32)
        denominator = jnp.exp(-row_top) + jnp.sum(chances, axis=-1)
        numerator = jnp.einsum("hqk,khd->qhd", chances, value_heads)
        result = numerator / jnp.transpose(denominator)[..., None]
        return result.reshape(block_rows, HEADS * HEAD_DIM).astype(jnp.bfloat16)

    attended = lax.map(attend_block, queries.reshape(TOKENS // block_rows, block_rows, HEADS * HEAD_DIM))
    attended = attended.reshape(TOKENS, HEADS * HEAD_DIM)
    return jnp.dot(attended, out_weight, preferred_element_type=jnp.float32).astype(jnp.bfloat16)
```

```python
import functools

import jax
import jax.numpy as jnp
from jax import lax
from jax.experimental import pallas as pl
from jax.experimental.pallas import tpu as pltpu
from jax.sharding import PartitionSpec as P

HEAD_DIM = 64
GROUPS = 4
LANES = 128
MARK = 100.0
MARK_TEST = 64.0
SAFE = 64.0
LOW = -1e30
BF16 = jnp.bfloat16
F32 = jnp.float32
VMEM = pl.BlockSpec(memory_space=pltpu.VMEM)
NT = (((1,), (1,)), ((), ()))


def params():
    return pltpu.CompilerParams(vmem_limit_bytes=48 * 1024 * 1024)


def lower_lanes(shape):
    return lax.broadcasted_iota(jnp.int32, shape, 1) < HEAD_DIM


def swap_halves(x):
    return pltpu.roll(x, HEAD_DIM, 1)


def pack_kernel(rest, per_group, q_ref, k_ref, v_ref, valid_ref, *outs):
    mine = lax.axis_index("inner") // rest
    rows = q_ref.shape[0]
    half = rows // 2
    square = (rows, rows)
    on_diagonal = lax.broadcasted_iota(jnp.int32, square, 0) == lax.broadcasted_iota(
        jnp.int32, square, 1
    )
    flag_row = jnp.broadcast_to(valid_ref[...].astype(F32), square)
    picked = jnp.where(on_diagonal, flag_row, 0.0).astype(BF16)
    flags = jnp.dot(picked, jnp.ones((rows, LANES), BF16), preferred_element_type=F32) > 0.5
    low = lower_lanes((rows, LANES))
    low_half = lower_lanes((half, LANES))
    kv_groups, q_groups = [], []
    for g in range(GROUPS):
        kv_slots, q_slots = [], []
        for j in range(per_group):
            h = g * per_group + j
            tile = pl.ds((h // 2) * LANES, LANES)
            k = k_ref[:, tile].astype(F32)
            v = v_ref[:, tile].astype(F32)
            q = q_ref[:, tile].astype(F32) * (HEAD_DIM**-0.5)
            if h % 2 == 0:
                kv = jnp.where(low, k, swap_halves(v))
                qq = jnp.where(low_half, q[:half], swap_halves(q[half:]))
            else:
                kv = jnp.where(low, swap_halves(k), v)
                qq = jnp.where(low_half, swap_halves(q[:half]), q[half:])
            kv_slots.append(jnp.where(flags, kv, MARK))
            q_slots.append(qq)
        kv_groups.append(kv_slots)
        q_groups.append(q_slots)
    for s in range(GROUPS):
        want = lax.rem(mine + s, GROUPS)
        for j in range(per_group):
            lanes = pl.ds(j * LANES, LANES)
            for groups, out in ((kv_groups, outs[s]), (q_groups, outs[GROUPS + s])):
                x = groups[0][j]
                for g in range(1, GROUPS):
                    x = jnp.where(want == g, groups[g][j], x)
                out[:, lanes] = x.astype(BF16)


def pack(q, k, v, valid, rest):
    rows, width = q.shape
    per_group = width // HEAD_DIM // GROUPS
    slots = per_group * LANES
    return pl.pallas_call(
        functools.partial(pack_kernel, rest, per_group),
        out_shape=[jax.ShapeDtypeStruct((rows, slots), BF16)] * GROUPS
        + [jax.ShapeDtypeStruct((rows // 2, slots), BF16)] * GROUPS,
        in_specs=[VMEM] * 4,
        out_specs=[VMEM] * (2 * GROUPS),
        compiler_params=params(),
    )(q, k, v, valid.reshape(1, rows))


def attend_kernel(n_q, n_kv, half, first, *refs):
    q_refs, refs = refs[:n_q], refs[n_q:]
    kv_refs, refs = refs[:n_kv], refs[n_kv:]
    if not first:
        acc_in, top_in = refs[:2]
        refs = refs[2:]
    acc, top, qs, ks, vs = refs
    slots = qs.shape[1] // LANES
    rows_q = qs.shape[0]
    rows_k = ks.shape[0]
    start = 0
    for ref in q_refs:
        for piece in range(ref.shape[0] // half):
            for j in range(slots):
                lanes = pl.ds(j * LANES, LANES)
                x = ref[pl.ds(piece * half, half), lanes].astype(F32)
                low = lower_lanes(x.shape)
                qs[pl.ds(start, half), lanes] = jnp.where(low, x, 0.0).astype(BF16)
                qs[pl.ds(start + half, half), lanes] = jnp.where(low, swap_halves(x), 0.0).astype(BF16)
            start += 2 * half
    start = 0
    for ref in kv_refs:
        n = ref.shape[0]
        for j in range(slots):
            lanes = pl.ds(j * LANES, LANES)
            x = ref[:, lanes].astype(F32)
            hole = x > MARK_TEST
            low = lower_lanes(x.shape)
            x = jnp.where(hole, 0.0, x)
            ks[pl.ds(start, n), lanes] = x.astype(BF16)
            vs[pl.ds(start, n), lanes] = jnp.where(low, jnp.where(hole, 0.0, 1.0), x).astype(BF16)
        start += n
    pick = (lax.broadcasted_iota(jnp.int32, (LANES, LANES), 0) < HEAD_DIM).astype(BF16)

    def largest(ref):
        best = None
        for j in range(slots):
            x = ref[:, pl.ds(j * LANES, LANES)].astype(F32)
            norms = jnp.dot((x * x).astype(BF16), pick, preferred_element_type=F32)
            best = norms if best is None else jnp.maximum(best, norms)
        return jnp.max(best)

    bound = largest(qs) * largest(ks) * 1.05
    safe = bound <= SAFE * SAFE
    if first:
        top[...] = jnp.zeros_like(top)
        acc[...] = jnp.zeros_like(acc)
    else:
        safe = jnp.logical_and(safe, jnp.max(top_in[...]) == 0.0)
        top[...] = top_in[...]
        acc[...] = acc_in[...]
    block = min(256, rows_q)

    @pl.when(safe)
    def _():
        for j in range(slots):
            lanes = pl.ds(j * LANES, LANES)
            for r in range(0, rows_q, block):
                at = pl.ds(r, block)
                s = lax.dot_general(qs[at, lanes], ks[:, lanes], NT, preferred_element_type=F32)
                p = jnp.exp(s).astype(BF16)
                acc[at, lanes] = acc[at, lanes] + jnp.dot(p, vs[:, lanes], preferred_element_type=F32)

    @pl.when(jnp.logical_not(safe))
    def _():
        step_q, step_k = 128, 256

        def over_queries(i, unused):
            at = pl.ds(pl.multiple_of(i * step_q, step_q), step_q)
            lane = lax.broadcasted_iota(jnp.int32, (step_q, LANES), 1)
            tops = top[at, :]
            for j in range(slots):
                lanes = pl.ds(j * LANES, LANES)
                own = jnp.sum(jnp.where(lane == j, tops, 0.0), axis=1, keepdims=True)

                def over_keys(c, carry):
                    high, total = carry
                    ka = pl.ds(pl.multiple_of(c * step_k, step_k), step_k)
                    s = lax.dot_general(qs[at, lanes], ks[ka, lanes], NT, preferred_element_type=F32)
                    ones = lax.dot_general(
                        jnp.ones((step_q, LANES), BF16),
                        jnp.where(lower_lanes((step_k, LANES)), vs[ka, lanes].astype(F32), 0.0).astype(BF16),
                        NT,
                        preferred_element_type=F32,
                    )
                    s = jnp.where(ones > 0.5, s, LOW)
                    new = jnp.maximum(high, jnp.max(s, axis=1, keepdims=True))
                    p = jnp.exp(s - new).astype(BF16)
                    total = total * jnp.exp(high - new) + jnp.dot(p, vs[ka, lanes], preferred_element_type=F32)
                    return new, total

                high, total = lax.fori_loop(0, rows_k // step_k, over_keys, (own, acc[at, lanes]))
                acc[at, lanes] = total
                tops = jnp.where(lane == j, high, tops)
            top[at, :] = tops
            return unused

        lax.fori_loop(0, rows_q // step_q, over_queries, 0)


def attend(q_list, kv_list, half, state):
    slots = q_list[0].shape[1]
    rows_q = 2 * sum(q.shape[0] for q in q_list)
    rows_k = sum(k.shape[0] for k in kv_list)
    first = state is None
    args = list(q_list) + list(kv_list) + ([] if first else list(state))
    return pl.pallas_call(
        functools.partial(attend_kernel, len(q_list), len(kv_list), half, first),
        out_shape=[
            jax.ShapeDtypeStruct((rows_q, slots), F32),
            jax.ShapeDtypeStruct((rows_q, LANES), F32),
        ],
        in_specs=[VMEM] * len(args),
        out_specs=[VMEM] * 2,
        scratch_shapes=[
            pltpu.VMEM((rows_q, slots), BF16),
            pltpu.VMEM((rows_k, slots), BF16),
            pltpu.VMEM((rows_k, slots), BF16),
        ],
        compiler_params=params(),
        cost_estimate=pl.CostEstimate(
            flops=4 * rows_q * rows_k * slots, bytes_accessed=4 * rows_q * slots, transcendentals=rows_q * rows_k * slots // LANES
        ),
    )(*args)


def settle_kernel(n, *refs):
    accs, tops, outs = refs[:n], refs[n : 2 * n], refs[2 * n :]
    rows, width = accs[0].shape
    slots = width // LANES
    lane = lax.broadcasted_iota(jnp.int32, (rows, LANES), 1)
    piece = rows // len(outs)
    half = piece // 2
    low_half = lower_lanes((half, LANES))
    for j in range(slots):
        lanes = pl.ds(j * LANES, LANES)
        own = [jnp.sum(jnp.where(lane == j, t[...], 0.0), axis=1, keepdims=True) for t in tops]
        high = functools.reduce(jnp.maximum, own)
        total = functools.reduce(lambda a, b: a + b, [a[:, lanes] * jnp.exp(t - high) for a, t in zip(accs, own)])
        result = total / (swap_halves(total) + jnp.exp(-high))
        for i, out in enumerate(outs):
            first = result[i * piece : i * piece + half]
            second = result[i * piece + half : (i + 1) * piece]
            out[:, lanes] = jnp.where(low_half, swap_halves(first), second).astype(BF16)


def settle(accs, tops, n_out):
    rows, width = accs[0].shape
    return pl.pallas_call(
        functools.partial(settle_kernel, len(accs)),
        out_shape=[jax.ShapeDtypeStruct((rows // n_out // 2, width), BF16)] * n_out,
        in_specs=[VMEM] * (2 * len(accs)),
        out_specs=[VMEM] * n_out,
        compiler_params=params(),
    )(*accs, *tops)


def project_kernel(rest, *refs):
    parts, w_ref, out, joined = refs[:GROUPS], refs[GROUPS], refs[GROUPS + 1], refs[GROUPS + 2]
    mine = lax.axis_index("inner") // rest
    half, width = parts[0].shape
    slots = width // LANES
    group_rows = slots * HEAD_DIM
    total = None
    for s, part in enumerate(parts):
        for j in range(slots):
            x = part[:, pl.ds(j * LANES, LANES)]
            joined[:half, pl.ds(j * HEAD_DIM, HEAD_DIM)] = x[:, :HEAD_DIM]
            joined[half:, pl.ds(j * HEAD_DIM, HEAD_DIM)] = x[:, HEAD_DIM:]
        g = lax.rem(mine + s, GROUPS)
        w = w_ref[pl.ds(pl.multiple_of(g * group_rows, 16), group_rows), :]
        term = jnp.dot(joined[...], w, preferred_element_type=F32)
        total = term if total is None else total + term
    out[...] = total.astype(BF16)


def project(parts, w, rest):
    half, width = parts[0].shape
    return pl.pallas_call(
        functools.partial(project_kernel, rest),
        out_shape=jax.ShapeDtypeStruct((2 * half, w.shape[1]), BF16),
        in_specs=[VMEM] * (GROUPS + 1),
        out_specs=VMEM,
        scratch_shapes=[pltpu.VMEM((2 * half, width // 2), BF16)],
        compiler_params=params(),
    )(*parts, w)


def on_device(n_blk, n_inner, q, k, v, valid, w):
    rest = n_inner // GROUPS

    def over_groups(x, s):
        return lax.ppermute(x, "inner", [(i, (i + s * rest) % n_inner) for i in range(n_inner)])

    def over_rest(x, t):
        return lax.ppermute(x, "inner", [(i, i // rest * rest + (i + t) % rest) for i in range(n_inner)])

    def over_blk(x, move):
        return lax.ppermute(x, "blk", [(i, move(i)) for i in range(n_blk)])

    def spread(chunk, which):
        if n_blk == 4:
            from_x = over_blk(chunk, lambda i: i ^ 1)
            from_y = over_blk(chunk, lambda i: i ^ 2)
            if which == 0:
                far = over_blk(from_y, lambda i: i ^ 1)
            else:
                far = over_blk(from_x, lambda i: i ^ 2)
            return [chunk, from_x, from_y, far]
        return [chunk] + [over_blk(chunk, lambda i, t=t: (i + t) % n_blk) for t in range(1, n_blk)]

    packed = pack(q, k, v, valid, rest)
    kv, qs = packed[:GROUPS], packed[GROUPS:]
    kv = [kv[0]] + [over_groups(kv[s], s) for s in range(1, GROUPS)]
    qs = [qs[0]] + [over_groups(qs[s], s) for s in range(1, GROUPS)]
    blocks = spread(jnp.concatenate(kv[:2], axis=0), 0) + spread(jnp.concatenate(kv[2:], axis=0), 1)
    q_own = jnp.concatenate(qs, axis=0)
    q_list = [q_own] + [over_rest(q_own, t) for t in range(1, rest)]
    acc, top = attend(q_list, blocks, q.shape[0] // 2, None)
    rows = 2 * q_own.shape[0]
    accs, tops = [acc[:rows]], [top[:rows]]
    for t in range(1, rest):
        accs.append(over_rest(acc[t * rows : (t + 1) * rows], rest - t))
        tops.append(over_rest(top[t * rows : (t + 1) * rows], rest - t))
    parts = settle(accs, tops, GROUPS)
    parts = [parts[0]] + [over_groups(parts[s], GROUPS - s) for s in range(1, GROUPS)]
    return project(parts, w, rest)


def solution(mesh):
    rows = P(("blk", "inner"), None)
    return jax.shard_map(
        functools.partial(on_device, mesh.shape["blk"], mesh.shape["inner"]),
        mesh=mesh,
        in_specs=(rows, rows, rows, P(("blk", "inner")), P()),
        out_specs=rows,
        check_vma=False,
    )
```

```python
import functools

import jax
import jax.numpy as jnp
from jax import lax
from jax.experimental import pallas as pl
from jax.experimental.pallas import tpu as pltpu
from jax.sharding import PartitionSpec as P

HEAD_DIM = 64
GROUPS = 4
LANES = 128
MARK = 100.0
MARK_TEST = 64.0
SAFE = 64.0
LOW = -1e30
ONES = 16
MOST_QUERIES = 1024
MOST_KEYS = 2048
LIMIT = 1e30
BF16 = jnp.bfloat16
F32 = jnp.float32
VMEM = pl.BlockSpec(memory_space=pltpu.VMEM)
NT = (((1,), (1,)), ((), ()))
TN = (((0,), (0,)), ((), ()))


MIB = 1024 * 1024


def params(mib=32):
    return pltpu.CompilerParams(vmem_limit_bytes=mib * MIB)


def lower_lanes(shape):
    return lax.broadcasted_iota(jnp.int32, shape, 1) < HEAD_DIM


def swap_halves(x):
    return pltpu.roll(x, HEAD_DIM, 1)


def pack_kernel(rest, per_group, q_hbm, k_hbm, v_hbm, valid_hbm, *refs):
    outs, (q_ref, k_ref, v_ref, valid_ref, sems) = refs[:GROUPS], refs[GROUPS:]
    copies = [
        pltpu.make_async_copy(src, dst, sems.at[i])
        for i, (src, dst) in enumerate(
            ((valid_hbm, valid_ref), (k_hbm, k_ref), (v_hbm, v_ref), (q_hbm, q_ref))
        )
    ]
    for copy in copies:
        copy.start()
    mine = lax.axis_index("inner") // rest
    rows = q_ref.shape[0]
    half = rows // 2
    for copy in copies:
        copy.wait()
    square = (rows, rows)
    on_diagonal = lax.broadcasted_iota(jnp.int32, square, 0) == lax.broadcasted_iota(
        jnp.int32, square, 1
    )
    flag_row = jnp.broadcast_to(valid_ref[...].astype(F32), square)
    picked = jnp.where(on_diagonal, flag_row, 0.0).astype(BF16)
    flags = jnp.dot(picked, jnp.ones((rows, LANES), BF16), preferred_element_type=F32) > 0.5
    low = lower_lanes((rows, LANES))
    low_half = lower_lanes((half, LANES))
    kv_groups, q_groups = [], []
    for g in range(GROUPS):
        kv_slots, q_slots = [], []
        for j in range(per_group):
            h = g * per_group + j
            tile = pl.ds((h // 2) * LANES, LANES)
            k = k_ref[:, tile].astype(F32)
            v = v_ref[:, tile].astype(F32)
            q = q_ref[:, tile].astype(F32) * (HEAD_DIM**-0.5)
            if h % 2 == 0:
                kv = jnp.where(low, k, swap_halves(v))
                qq = jnp.where(low_half, q[:half], swap_halves(q[half:]))
            else:
                kv = jnp.where(low, swap_halves(k), v)
                qq = jnp.where(low_half, swap_halves(q[:half]), q[half:])
            kv_slots.append(jnp.where(flags, kv, MARK))
            q_slots.append(qq)
        kv_groups.append(kv_slots)
        q_groups.append(q_slots)
    for s in range(GROUPS):
        want = lax.rem(mine + s, GROUPS)
        for j in range(per_group):
            lanes = pl.ds(j * LANES, LANES)
            for groups, start, n in ((kv_groups, 0, rows), (q_groups, rows, half)):
                x = groups[0][j]
                for g in range(1, GROUPS):
                    x = jnp.where(want == g, groups[g][j], x)
                outs[s][pl.ds(start, n), lanes] = x.astype(BF16)


def pack(q, k, v, valid, rest):
    rows, width = q.shape
    per_group = width // HEAD_DIM // GROUPS
    slots = per_group * LANES
    return pl.pallas_call(
        functools.partial(pack_kernel, rest, per_group),
        out_shape=[jax.ShapeDtypeStruct((rows + rows // 2, slots), BF16)] * GROUPS,
        in_specs=[pl.BlockSpec(memory_space=pltpu.HBM)] * 4,
        out_specs=[VMEM] * GROUPS,
        scratch_shapes=[pltpu.VMEM((rows, width), BF16)] * 3
        + [pltpu.VMEM((1, rows), jnp.int32), pltpu.SemaphoreType.DMA((4,))],
        compiler_params=params(24),
    )(*[pltpu.with_memory_space_constraint(x, pltpu.HBM) for x in (q, k, v, valid.reshape(1, rows))])


def spread_queries(refs, half, qs):
    start = 0
    for ref in refs:
        for piece in range(ref.shape[0] // half):
            for j in range(qs.shape[1] // LANES):
                lanes = pl.ds(j * LANES, LANES)
                x = ref[pl.ds(piece * half, half), lanes].astype(F32)
                low = lower_lanes(x.shape)
                qs[pl.ds(start, half), lanes] = jnp.where(low, x, 0.0).astype(BF16)
                qs[pl.ds(start + half, half), lanes] = jnp.where(low, swap_halves(x), 0.0).astype(BF16)
            start += 2 * half


def spread_keys(refs, ks, vs):
    start = 0
    for ref in refs:
        n = ref.shape[0]
        for j in range(ks.shape[1] // LANES):
            lanes = pl.ds(j * LANES, LANES)
            x = ref[:, lanes]
            hole = x > jnp.asarray(MARK_TEST, BF16)
            low = lower_lanes(x.shape)
            zero = jnp.zeros_like(x)
            x = jnp.where(hole, zero, x)
            ks[pl.ds(start, n), lanes] = x
            vs[pl.ds(start, n), lanes] = jnp.where(low, jnp.where(hole, zero, jnp.ones_like(x)), x)
        start += n


def largest_norm(ref):
    pick = (lax.broadcasted_iota(jnp.int32, (LANES, LANES), 0) < HEAD_DIM).astype(BF16)
    best = None
    for j in range(ref.shape[1] // LANES):
        x = ref[:, pl.ds(j * LANES, LANES)]
        norms = jnp.dot(x * x, pick, preferred_element_type=F32)
        best = norms if best is None else jnp.maximum(best, norms)
    return jnp.max(best, axis=0, keepdims=True)[0, 0]


def add_keys(cols, qs, ks, vs, acc, top, safe, fresh):
    slots = ks.shape[1] // LANES
    rows_k = ks.shape[0]

    @pl.when(safe)
    def _():
        for j in range(slots):
            lanes = pl.ds(j * LANES, LANES)
            for col in range(0, cols, MOST_QUERIES):
                at = pl.ds(col, min(MOST_QUERIES, cols - col))
                total = None if fresh else acc[lanes, at]
                for row in range(0, rows_k, MOST_KEYS):
                    ka = pl.ds(row, min(MOST_KEYS, rows_k - row))
                    s = lax.dot_general(ks[ka, lanes], qs[at, lanes], NT, preferred_element_type=F32)
                    p = jnp.exp(s).astype(BF16)
                    term = lax.dot_general(vs[ka, lanes], p, TN, preferred_element_type=F32)
                    total = term if total is None else total + term
                acc[lanes, at] = total

    @pl.when(jnp.logical_not(safe))
    def _():
        step_q, step_k = 128, 128
        if fresh:
            acc[...] = jnp.zeros_like(acc)

        def over_queries(i, unused):
            at = pl.ds(pl.multiple_of(i * step_q, step_q), step_q)
            for j in range(slots):
                lanes = pl.ds(j * LANES, LANES)

                def over_keys(c, carry):
                    high, total = carry
                    ka = pl.ds(pl.multiple_of(c * step_k, step_k), step_k)
                    v = vs[ka, lanes]
                    s = lax.dot_general(ks[ka, lanes], qs[at, lanes], NT, preferred_element_type=F32)
                    s = jnp.where(v[:, :1].astype(F32) > 0.5, s, LOW)
                    best = jnp.max(s, axis=0, keepdims=True)
                    best = (best + jnp.abs(best) * (1.0 / 128)).astype(BF16).astype(F32)
                    new = jnp.maximum(high, best)
                    p = jnp.exp(s - new).astype(BF16)
                    total = total * jnp.exp(high - new) + lax.dot_general(v, p, TN, preferred_element_type=F32)
                    return new, total

                high, total = lax.fori_loop(0, rows_k // step_k, over_keys, (top[pl.ds(j, 1), at], acc[lanes, at]))
                acc[lanes, at] = total
                top[pl.ds(j, 1), at] = high
            return unused

        lax.fori_loop(0, cols // step_q, over_queries, 0)


def attend_kernel(n_q, n_kv, half, first, n_export, *refs):
    q_refs, refs = refs[:n_q], refs[n_q:]
    kv_refs, refs = refs[:n_kv], refs[n_kv:]
    if first:
        qs, acc, top, info = refs[:4]
        exports, (ks, vs) = refs[4 : 4 + n_export], refs[4 + n_export :]
        spread_queries(q_refs, half, qs)
        top[...] = jnp.zeros_like(top)
        length = largest_norm(qs)
    else:
        qs = q_refs[0]
        unused_acc, unused_top, info_in, acc, top, info = refs[:6]
        exports, (ks, vs) = refs[6 : 6 + n_export], refs[6 + n_export :]
        length = info_in[...][0, 0]
    spread_keys(kv_refs, ks, vs)
    safe = length * largest_norm(ks) * 1.05 <= SAFE * SAFE
    info[...] = jnp.full(info.shape, jnp.where(safe, length, LIMIT), F32)
    add_keys(qs.shape[0], qs, ks, vs, acc, top, safe, first)
    cols = qs.shape[0] // (n_export + 1)
    for i, out in enumerate(exports):
        at = pl.ds((i + 1) * cols, cols)
        for j in range(qs.shape[1] // LANES):
            start = j * (HEAD_DIM + 2 * ONES)
            out[pl.ds(start, HEAD_DIM), :] = acc[pl.ds(j * LANES + HEAD_DIM, HEAD_DIM), at].astype(BF16)
            out[pl.ds(start + HEAD_DIM, ONES), :] = acc[pl.ds(j * LANES, ONES), at].astype(BF16)
            shift = jnp.broadcast_to(top[pl.ds(j, 1), at], (ONES, cols))
            out[pl.ds(start + HEAD_DIM + ONES, ONES), :] = shift.astype(BF16)


def attend(q_list, kv_list, half, state, n_export=0):
    width = q_list[0].shape[1]
    slots = width // LANES
    first = state is None
    rows_q = sum(q.shape[0] for q in q_list) * (2 if first else 1)
    rows_k = sum(k.shape[0] for k in kv_list)
    args = list(q_list) + list(kv_list) + ([] if first else list(state))
    out_shape = [jax.ShapeDtypeStruct((rows_q, width), BF16)] if first else []
    out_shape += [
        jax.ShapeDtypeStruct((width, rows_q), F32),
        jax.ShapeDtypeStruct((8, rows_q), F32),
        jax.ShapeDtypeStruct((8, LANES), F32),
    ]
    sent = (slots * (HEAD_DIM + 2 * ONES), rows_q // (n_export + 1))
    out_shape += [jax.ShapeDtypeStruct(sent, BF16)] * n_export
    out = pl.pallas_call(
        functools.partial(attend_kernel, len(q_list), len(kv_list), half, first, n_export),
        out_shape=out_shape,
        in_specs=[VMEM] * len(args),
        out_specs=[VMEM] * len(out_shape),
        scratch_shapes=[pltpu.VMEM((rows_k, width), BF16)] * 2,
        input_output_aliases={} if first else {len(args) - 3: 0, len(args) - 2: 1},
        compiler_params=params(),
        cost_estimate=pl.CostEstimate(
            flops=16 * rows_q * rows_k * width,
            bytes_accessed=4 * rows_q * width,
            transcendentals=rows_q * rows_k * slots,
        ),
    )(*args)
    out = list(out) if first else [q_list[0]] + list(out)
    return out[0], out[1:4], out[4:]


def finish_kernel(n_import, slots, acc, top, *refs):
    imports, outs = refs[:n_import], refs[n_import:]
    piece = outs[0].shape[1]
    step = HEAD_DIM + 2 * ONES
    for i, out in enumerate(outs):
        at = pl.ds(i * piece, piece)
        for j in range(slots):
            total = acc[pl.ds(j * LANES + HEAD_DIM, HEAD_DIM), at]
            count = acc[pl.ds(j * LANES, 1), at]
            high = top[pl.ds(j, 1), at]
            for ref in imports:
                values = ref[pl.ds(j * step, HEAD_DIM), at].astype(F32)
                sums = ref[pl.ds(j * step + HEAD_DIM, ONES), at].astype(F32)[:1]
                shift = ref[pl.ds(j * step + HEAD_DIM + ONES, ONES), at].astype(F32)[:1]
                new = jnp.maximum(high, shift)
                mine, theirs = jnp.exp(high - new), jnp.exp(shift - new)
                total = total * mine + values * theirs
                count = count * mine + sums * theirs
                high = new
            share = 1.0 / (count + jnp.exp(-high))
            out[pl.ds(j * HEAD_DIM, HEAD_DIM), :] = (total * share).astype(BF16)


def finish(state, imports, n_out):
    acc, top, unused = state
    slots = acc.shape[0] // LANES
    piece = acc.shape[1] // (len(imports) + 1) // n_out
    return pl.pallas_call(
        functools.partial(finish_kernel, len(imports), slots),
        out_shape=[jax.ShapeDtypeStruct((slots * HEAD_DIM, piece), BF16)] * n_out,
        in_specs=[VMEM] * (2 + len(imports)),
        out_specs=[VMEM] * n_out,
        compiler_params=params(),
    )(acc, top, *imports)


def project_kernel(rest, *refs):
    parts, w_ref, out = refs[:GROUPS], refs[GROUPS], refs[GROUPS + 1]
    mine = lax.axis_index("inner") // rest
    rows = parts[0].shape[0]
    total = None
    for s, part in enumerate(parts):
        g = lax.rem(mine + s, GROUPS)
        w = w_ref[pl.ds(pl.multiple_of(g * rows, 16), rows), :]
        term = lax.dot_general(part[...], w, TN, preferred_element_type=F32)
        total = term if total is None else total + term
    out[...] = total.astype(BF16)


def project(parts, w, rest):
    return pl.pallas_call(
        functools.partial(project_kernel, rest),
        out_shape=jax.ShapeDtypeStruct((parts[0].shape[1], w.shape[1]), BF16),
        in_specs=[VMEM] * (GROUPS + 1),
        out_specs=VMEM,
        compiler_params=params(),
    )(*parts, w)


def on_device(n_blk, n_inner, q, k, v, valid, w):
    rest = n_inner // GROUPS
    half = q.shape[0] // 2

    def over_groups(x, s):
        return lax.ppermute(x, "inner", [(i, (i + s * rest) % n_inner) for i in range(n_inner)])

    def over_rest(x, t):
        return lax.ppermute(x, "inner", [(i, i // rest * rest + (i + t) % rest) for i in range(n_inner)])

    def over_blk(x, t):
        return lax.ppermute(x, "blk", [(i, (i + t) % n_blk) for i in range(n_blk)])

    def along(first, second):
        return [
            (b * n_inner + i, (b ^ (second if i % 2 else first)) * n_inner + i)
            for b in range(n_blk)
            for i in range(n_inner)
        ]

    def near(chunk):
        return [lax.ppermute(chunk, ("blk", "inner"), along(d, d)) for d in (1, 2)]

    def passed(blocks):
        return jnp.where(lax.axis_index("inner") % 2 == 0, *blocks)

    def far(block):
        return lax.ppermute(block, ("blk", "inner"), along(2, 1))

    def after(x, *done):
        return lax.optimization_barrier((x, *done))[0]

    def diagonal(chunk):
        return lax.ppermute(chunk, ("blk", "inner"), along(3, 3))

    pieces = list(pack(q, k, v, valid, rest))
    rows = q.shape[0]

    def gathered_queries(pieces):
        own = jnp.concatenate([x[rows:] for x in pieces], axis=0)
        return [own] + [over_rest(own, t) for t in range(1, rest)]

    if n_blk == 4 and rest == 2:
        near0 = near(pieces[0][:rows])
        pieces[1], pieces[3] = over_groups(pieces[1], 1), over_groups(pieces[3], 3)
        pieces[2] = over_groups(after(pieces[2], pieces[1], pieces[3]), 2)
        chunk1 = jnp.concatenate([pieces[1][:rows], pieces[3][:rows]], axis=0)
        near1 = near(chunk1)
        far0 = far(passed(near0))
        near1 = after(tuple(near1), far0)
        far1 = far(passed(near1))
        chunk2 = after(pieces[2], *near1)[:rows]
        blocks2 = [*near(chunk2), diagonal(chunk2)]
        q_list = gathered_queries(pieces)
        chunks = [pieces[0][:rows], chunk1, chunk2]
        queries, state, unused = attend(q_list, [*chunks, *near0, far0, *near1], half, None)
        queries, state, exports = attend([queries], [far1, *blocks2], half, state, rest - 1)
    else:
        pieces = [pieces[0]] + [over_groups(pieces[s], s) for s in range(1, GROUPS)]
        kv = [x[:rows] for x in pieces]
        q_list = gathered_queries(pieces)
        chunk = jnp.concatenate(kv, axis=0)
        blocks = [chunk] + [over_blk(chunk, t) for t in range(1, n_blk)]
        queries, state, exports = attend(q_list, blocks, half, None, rest - 1)
    imports = [over_rest(x, rest - 1 - t) for t, x in enumerate(exports)]
    parts = list(finish(state, imports, GROUPS))
    parts = [parts[0]] + [over_groups(parts[s], GROUPS - s) for s in range(1, GROUPS)]
    return project(parts, w, rest)


def solution(mesh):
    rows = P(("blk", "inner"), None)
    return jax.shard_map(
        functools.partial(on_device, mesh.shape["blk"], mesh.shape["inner"]),
        mesh=mesh,
        in_specs=(rows, rows, rows, P(("blk", "inner")), P()),
        out_specs=rows,
        check_vma=False,
    )
```

```python
import functools

import jax
import jax.numpy as jnp
from jax import lax
from jax.experimental import pallas as pl
from jax.experimental.pallas import tpu as pltpu
from jax.sharding import PartitionSpec as P

HEAD_DIM = 64
GROUPS = 4
LANES = 128
MARK = 100.0
MARK_TEST = 64.0
SAFE = 64.0
LOW = -1e30
ONES = 16
MOST_QUERIES = 1024
MOST_KEYS = 2048
LIMIT = 1e30
BF16 = jnp.bfloat16
F32 = jnp.float32
VMEM = pl.BlockSpec(memory_space=pltpu.VMEM)
NT = (((1,), (1,)), ((), ()))
TN = (((0,), (0,)), ((), ()))


MIB = 1024 * 1024


def params(mib=32):
    return pltpu.CompilerParams(vmem_limit_bytes=mib * MIB)


def lower_lanes(shape):
    return lax.broadcasted_iota(jnp.int32, shape, 1) < HEAD_DIM


def swap_halves(x):
    return pltpu.roll(x, HEAD_DIM, 1)


def pack_kernel(rest, per_group, q_hbm, k_hbm, v_hbm, valid_hbm, *refs):
    outs, (q_ref, k_ref, v_ref, valid_ref, sems) = refs[:GROUPS], refs[GROUPS:]
    copies = [
        pltpu.make_async_copy(src, dst, sems.at[i])
        for i, (src, dst) in enumerate(
            ((valid_hbm, valid_ref), (k_hbm, k_ref), (v_hbm, v_ref), (q_hbm, q_ref))
        )
    ]
    for copy in copies:
        copy.start()
    mine = lax.axis_index("inner") // rest
    rows = q_ref.shape[0]
    half = rows // 2
    for copy in copies:
        copy.wait()
    square = (rows, rows)
    on_diagonal = lax.broadcasted_iota(jnp.int32, square, 0) == lax.broadcasted_iota(
        jnp.int32, square, 1
    )
    flag_row = jnp.broadcast_to(valid_ref[...].astype(F32), square)
    picked = jnp.where(on_diagonal, flag_row, 0.0).astype(BF16)
    flags = jnp.dot(picked, jnp.ones((rows, LANES), BF16), preferred_element_type=F32) > 0.5
    low = lower_lanes((rows, LANES))
    low_half = lower_lanes((half, LANES))
    kv_groups, q_groups = [], []
    for g in range(GROUPS):
        kv_slots, q_slots = [], []
        for j in range(per_group):
            h = g * per_group + j
            tile = pl.ds((h // 2) * LANES, LANES)
            k = k_ref[:, tile].astype(F32)
            v = v_ref[:, tile].astype(F32)
            q = q_ref[:, tile].astype(F32) * (HEAD_DIM**-0.5)
            if h % 2 == 0:
                kv = jnp.where(low, k, swap_halves(v))
                qq = jnp.where(low_half, q[:half], swap_halves(q[half:]))
            else:
                kv = jnp.where(low, swap_halves(k), v)
                qq = jnp.where(low_half, swap_halves(q[:half]), q[half:])
            kv_slots.append(jnp.where(flags, kv, MARK))
            q_slots.append(qq)
        kv_groups.append(kv_slots)
        q_groups.append(q_slots)
    for s in range(GROUPS):
        want = jnp.bitwise_xor(mine, s)
        for j in range(per_group):
            lanes = pl.ds(j * LANES, LANES)
            for groups, start, n in ((kv_groups, 0, rows), (q_groups, rows, half)):
                x = groups[0][j]
                for g in range(1, GROUPS):
                    x = jnp.where(want == g, groups[g][j], x)
                outs[s][pl.ds(start, n), lanes] = x.astype(BF16)


def pack(q, k, v, valid, rest):
    rows, width = q.shape
    per_group = width // HEAD_DIM // GROUPS
    slots = per_group * LANES
    return pl.pallas_call(
        functools.partial(pack_kernel, rest, per_group),
        out_shape=[jax.ShapeDtypeStruct((rows + rows // 2, slots), BF16)] * GROUPS,
        in_specs=[pl.BlockSpec(memory_space=pltpu.HBM)] * 4,
        out_specs=[VMEM] * GROUPS,
        scratch_shapes=[pltpu.VMEM((rows, width), BF16)] * 3
        + [pltpu.VMEM((1, rows), jnp.int32), pltpu.SemaphoreType.DMA((4,))],
        compiler_params=params(24),
    )(*[pltpu.with_memory_space_constraint(x, pltpu.HBM) for x in (q, k, v, valid.reshape(1, rows))])


def spread_queries(refs, half, qs):
    start = 0
    for ref in refs:
        for piece in range(ref.shape[0] // half):
            for j in range(qs.shape[1] // LANES):
                lanes = pl.ds(j * LANES, LANES)
                x = ref[pl.ds(piece * half, half), lanes].astype(F32)
                low = lower_lanes(x.shape)
                qs[pl.ds(start, half), lanes] = jnp.where(low, x, 0.0).astype(BF16)
                qs[pl.ds(start + half, half), lanes] = jnp.where(low, swap_halves(x), 0.0).astype(BF16)
            start += 2 * half


def spread_keys(refs, ks, vs):
    start = 0
    for ref in refs:
        n = ref.shape[0]
        for j in range(ks.shape[1] // LANES):
            lanes = pl.ds(j * LANES, LANES)
            x = ref[:, lanes]
            hole = x > jnp.asarray(MARK_TEST, BF16)
            low = lower_lanes(x.shape)
            zero = jnp.zeros_like(x)
            x = jnp.where(hole, zero, x)
            ks[pl.ds(start, n), lanes] = x
            vs[pl.ds(start, n), lanes] = jnp.where(low, jnp.where(hole, zero, jnp.ones_like(x)), x)
        start += n


def largest_norm(ref):
    pick = lower_lanes((16, LANES)).astype(BF16)
    best = None
    for j in range(ref.shape[1] // LANES):
        x = ref[:, pl.ds(j * LANES, LANES)]
        norms = lax.dot_general(pick, x * x, NT, preferred_element_type=F32)
        best = norms if best is None else jnp.maximum(best, norms)
    return jnp.max(best[:8])


def add_keys(work, ks, vs, safe):
    slots = ks.shape[1] // LANES
    rows_k = ks.shape[0]

    @pl.when(safe)
    def _():
        steps = []
        for first_key, fresh, qs, acc, unused in work:
            for j in range(slots):
                for col in range(0, qs.shape[0], MOST_QUERIES):
                    at = pl.ds(col, min(MOST_QUERIES, qs.shape[0] - col))
                    for row in range(first_key, rows_k, MOST_KEYS):
                        ka = pl.ds(row, min(MOST_KEYS, rows_k - row))
                        steps.append((qs, acc, pl.ds(j * LANES, LANES), at, ka, fresh and row == first_key))

        def scores(step):
            qs, unused, lanes, at, ka, unused = step
            return lax.dot_general(ks[ka, lanes], qs[at, lanes], NT, preferred_element_type=F32)

        ahead = scores(steps[0])
        for i, (qs, acc, lanes, at, ka, zero) in enumerate(steps):
            p = jnp.exp(ahead).astype(BF16)
            if i + 1 < len(steps):
                ahead = scores(steps[i + 1])
            term = lax.dot_general(vs[ka, lanes], p, TN, preferred_element_type=F32)
            acc[lanes, at] = term if zero else acc[lanes, at] + term

    @pl.when(jnp.logical_not(safe))
    def _():
        for first_key, fresh, qs, acc, top in work:
            if fresh:
                acc[...] = jnp.zeros_like(acc)
            add_keys_shifted(first_key, qs, ks, vs, acc, top)


def add_keys_shifted(first_key, qs, ks, vs, acc, top):
    slots = ks.shape[1] // LANES
    rows_k = ks.shape[0]
    cols = qs.shape[0]
    step_q, step_k = 128, 128

    def over_queries(i, unused):
        at = pl.ds(pl.multiple_of(i * step_q, step_q), step_q)
        for j in range(slots):
            lanes = pl.ds(j * LANES, LANES)

            def over_keys(c, carry):
                high, total = carry
                ka = pl.ds(pl.multiple_of(c * step_k, step_k), step_k)
                v = vs[ka, lanes]
                s = lax.dot_general(ks[ka, lanes], qs[at, lanes], NT, preferred_element_type=F32)
                s = jnp.where(v[:, :1].astype(F32) > 0.5, s, LOW)
                best = jnp.max(s, axis=0, keepdims=True)
                best = (best + jnp.abs(best) * (1.0 / 128)).astype(BF16).astype(F32)
                new = jnp.maximum(high, best)
                p = jnp.exp(s - new).astype(BF16)
                total = total * jnp.exp(high - new) + lax.dot_general(v, p, TN, preferred_element_type=F32)
                return new, total

            high, total = lax.fori_loop(first_key // step_k, rows_k // step_k, over_keys, (top[pl.ds(j, 1), at], acc[lanes, at]))
            acc[lanes, at] = total
            top[pl.ds(j, 1), at] = high
        return unused

    lax.fori_loop(0, cols // step_q, over_queries, 0)


def attend_kernel(sets, n_kv, half, first, n_export, *refs):
    given = []
    for n_q, unused in sets:
        count = n_q or 3
        given.append(refs[:count])
        refs = refs[count:]
    kv_refs, refs = refs[:n_kv], refs[n_kv:]
    if not first:
        info_in, refs = refs[0], refs[1:]
    held = []
    for (n_q, unused), mine in zip(sets, given):
        count = 3 if n_q else 2
        held.append(refs[:3] if n_q else (mine[0], *refs[:2]))
        refs = refs[count:]
    info, exports, (ks, vs) = refs[0], refs[1 : 1 + n_export], refs[1 + n_export :]
    length = None if first else info_in[...][0, 0]
    for (n_q, unused), mine, (qs, acc, top) in zip(sets, given, held):
        if n_q:
            spread_queries(mine, half, qs)
            top[...] = jnp.zeros_like(top)
            own = largest_norm(qs)
            length = own if length is None else jnp.maximum(length, own)
    spread_keys(kv_refs, ks, vs)
    safe = length * largest_norm(ks) * 1.05 <= SAFE * SAFE
    info[...] = jnp.full(info.shape, jnp.where(safe, length, LIMIT), F32)
    add_keys([(first_key, n_q > 0, *mine) for (n_q, first_key), mine in zip(sets, held)], ks, vs, safe)
    for i, out in enumerate(exports):
        place = 0
        for qs, acc, top in held:
            cols = qs.shape[0] // (n_export + 1)
            at, to = pl.ds((i + 1) * cols, cols), pl.ds(place, cols)
            for j in range(qs.shape[1] // LANES):
                start = j * (HEAD_DIM + 2 * ONES)
                out[pl.ds(start, HEAD_DIM), to] = acc[pl.ds(j * LANES + HEAD_DIM, HEAD_DIM), at].astype(BF16)
                out[pl.ds(start + HEAD_DIM, ONES), to] = acc[pl.ds(j * LANES, ONES), at].astype(BF16)
                shift = jnp.broadcast_to(top[pl.ds(j, 1), at], (ONES, cols))
                out[pl.ds(start + HEAD_DIM + ONES, ONES), to] = shift.astype(BF16)
            place += cols


def attend(sets, kv_list, half, info, n_export=0):
    width = kv_list[0].shape[1]
    slots = width // LANES
    first = info is None
    rows_k = sum(k.shape[0] for k in kv_list)
    args, meta, out_shape, aliases, work, own_cols = [], [], [], {}, 0, 0
    for items, first_key in sets:
        new = items[0].dtype == items[1].dtype
        cols = sum(q.shape[0] for q in items) * 2 if new else items[0].shape[0]
        meta.append((len(items) if new else 0, first_key))
        if new:
            out_shape.append(jax.ShapeDtypeStruct((cols, width), BF16))
        else:
            aliases[len(args) + 1], aliases[len(args) + 2] = len(out_shape), len(out_shape) + 1
        out_shape += [jax.ShapeDtypeStruct((width, cols), F32), jax.ShapeDtypeStruct((8, cols), F32)]
        args += items
        work += cols * (rows_k - first_key)
        own_cols += cols // (n_export + 1)
    args += kv_list
    if not first:
        args.append(info)
    out_shape.append(jax.ShapeDtypeStruct((8, LANES), F32))
    out_shape += [jax.ShapeDtypeStruct((slots * (HEAD_DIM + 2 * ONES), own_cols), BF16)] * n_export
    out = list(
        pl.pallas_call(
            functools.partial(attend_kernel, meta, len(kv_list), half, first, n_export),
            out_shape=out_shape,
            in_specs=[VMEM] * len(args),
            out_specs=[VMEM] * len(out_shape),
            scratch_shapes=[pltpu.VMEM((rows_k, width), BF16)] * 2,
            input_output_aliases=aliases,
            compiler_params=params(),
            cost_estimate=pl.CostEstimate(
                flops=16 * work * width, bytes_accessed=4 * rows_k * width, transcendentals=work * slots
            ),
        )(*args)
    )
    states = []
    for (items, unused), (n_q, unused) in zip(sets, meta):
        states.append([out.pop(0) if n_q else items[0], out.pop(0), out.pop(0)])
    return states, out[0], out[1:]


def finish_kernel(n_sets, n_import, wanted, *refs):
    held = [refs[2 * i : 2 * i + 2] for i in range(n_sets)]
    imports, outs = refs[2 * n_sets : 2 * n_sets + n_import], list(refs[2 * n_sets + n_import :])
    piece = outs[0].shape[1]
    step = HEAD_DIM + 2 * ONES
    place = 0
    for acc, top in held:
        cols = acc.shape[1] // (n_import + 1)
        for col in range(0, cols, piece):
            if (place + col) // piece not in wanted:
                continue
            out = outs.pop(0)
            at, there = pl.ds(col, piece), pl.ds(place + col, piece)
            for j in range(acc.shape[0] // LANES):
                total = acc[pl.ds(j * LANES + HEAD_DIM, HEAD_DIM), at]
                count = acc[pl.ds(j * LANES, 1), at]
                high = top[pl.ds(j, 1), at]
                for ref in imports:
                    values = ref[pl.ds(j * step, HEAD_DIM), there].astype(F32)
                    sums = ref[pl.ds(j * step + HEAD_DIM, ONES), there].astype(F32)[:1]
                    shift = ref[pl.ds(j * step + HEAD_DIM + ONES, ONES), there].astype(F32)[:1]
                    new = jnp.maximum(high, shift)
                    mine, theirs = jnp.exp(high - new), jnp.exp(shift - new)
                    total = total * mine + values * theirs
                    count = count * mine + sums * theirs
                    high = new
                share = 1.0 / (count + jnp.exp(-high))
                out[pl.ds(j * HEAD_DIM, HEAD_DIM), :] = (total * share).astype(BF16)
        place += cols


def finish(states, imports, n_pieces, wanted):
    sums = [x for state in states for x in state[1:]]
    slots = sums[0].shape[0] // LANES
    piece = sum(state[1].shape[1] for state in states) // (len(imports) + 1) // n_pieces
    return pl.pallas_call(
        functools.partial(finish_kernel, len(states), len(imports), wanted),
        out_shape=[jax.ShapeDtypeStruct((slots * HEAD_DIM, piece), BF16)] * len(wanted),
        in_specs=[VMEM] * (len(sums) + len(imports)),
        out_specs=[VMEM] * len(wanted),
        compiler_params=params(),
    )(*sums, *imports)


def project_kernel(rest, *refs):
    parts, w_ref, out = refs[:GROUPS], refs[GROUPS], refs[GROUPS + 1]
    mine = lax.axis_index("inner") // rest
    rows = parts[0].shape[0]
    total = None
    for s, part in enumerate(parts):
        g = jnp.bitwise_xor(mine, s)
        w = w_ref[pl.ds(pl.multiple_of(g * rows, 16), rows), :]
        term = lax.dot_general(part[...], w, TN, preferred_element_type=F32)
        total = term if total is None else total + term
    out[...] = total.astype(BF16)


def project(parts, w, rest):
    return pl.pallas_call(
        functools.partial(project_kernel, rest),
        out_shape=jax.ShapeDtypeStruct((parts[0].shape[1], w.shape[1]), BF16),
        in_specs=[VMEM] * (GROUPS + 1),
        out_specs=VMEM,
        compiler_params=params(),
    )(*parts, w)


def on_device(n_blk, n_inner, q, k, v, valid, w):
    rest = n_inner // GROUPS
    half = q.shape[0] // 2

    def over_groups(x, s):
        return lax.ppermute(x, "inner", [(i, (i // rest ^ s) * rest + i % rest) for i in range(n_inner)])

    def over_rest(x, t):
        return lax.ppermute(x, "inner", [(i, i // rest * rest + (i + t) % rest) for i in range(n_inner)])

    def over_blk(x, t):
        return lax.ppermute(x, "blk", [(i, (i + t) % n_blk) for i in range(n_blk)])

    def along(first, second):
        return [
            (b * n_inner + i, (b ^ (second if i % 2 else first)) * n_inner + i)
            for b in range(n_blk)
            for i in range(n_inner)
        ]

    def near(chunk):
        return [lax.ppermute(chunk, ("blk", "inner"), along(d, d)) for d in (1, 2)]

    def passed(blocks):
        return jnp.where(lax.axis_index("inner") % 2 == 0, *blocks)

    def far(block):
        return lax.ppermute(block, ("blk", "inner"), along(2, 1))

    def after(x, *done):
        return lax.optimization_barrier((x, *done))[0]

    def diagonal(chunk):
        return lax.ppermute(chunk, ("blk", "inner"), along(3, 3))

    pieces = list(pack(q, k, v, valid, rest))
    rows = q.shape[0]

    def gathered_queries(pieces):
        own = jnp.concatenate([x[rows:] for x in pieces], axis=0)
        return [own] + [over_rest(own, t) for t in range(1, rest)]

    if n_blk == 4 and rest == 2:
        own0 = pieces[0][:rows]
        near0 = near(own0)
        pieces[1], pieces[2] = over_groups(pieces[1], 1), over_groups(pieces[2], 2)
        pieces[3] = over_groups(after(pieces[3], pieces[1], pieces[2]), 3)
        pieces[1], pieces[2] = after((pieces[1], pieces[2]), *near0)
        q_early = gathered_queries(pieces[:3])
        near0 = after(tuple(near0), *q_early)
        own1 = after(jnp.concatenate([x[:rows] for x in pieces[1:3]], axis=0), *q_early)
        near1 = near(own1)
        far0 = far(passed(near0))
        early = [own0, own1, *near0, far0]
        (early_set,), info, unused = attend([(q_early, 0)], early, half, None)
        near1 = after(tuple(near1), early_set[1])
        pass1 = passed(near1)
        far1 = far(pass1)
        last = after(pieces[3], early_set[1])
        own2 = last[:rows]
        block2 = [*near(own2), diagonal(own2)]
        q_late = gathered_queries([last])
        met = sum(x.shape[0] for x in early)
        states, info, unused = attend([(early_set, met), (q_late, 0)], [*early, *near1, own2], half, info)
        states, info, exports = attend([(x, 0) for x in states], [far1, *block2], half, info, rest - 1)
    else:
        pieces = [pieces[0]] + [over_groups(pieces[s], s) for s in range(1, GROUPS)]
        chunk = jnp.concatenate([x[:rows] for x in pieces], axis=0)
        blocks = [chunk] + [over_blk(chunk, t) for t in range(1, n_blk)]
        states, info, exports = attend([(gathered_queries(pieces), 0)], blocks, half, None, rest - 1)
    imports = [over_rest(x, rest - 1 - t) for t, x in enumerate(exports)]
    there = [over_groups(x, s) for s, x in zip((2, 3), finish(states, imports, GROUPS, (2, 3)))]
    own, beside = finish(states, imports, GROUPS, (0, 1))
    parts = [own, over_groups(beside, 1), *there]
    return project(parts, w, rest)


def solution(mesh):
    rows = P(("blk", "inner"), None)
    return jax.shard_map(
        functools.partial(on_device, mesh.shape["blk"], mesh.shape["inner"]),
        mesh=mesh,
        in_specs=(rows, rows, rows, P(("blk", "inner")), P()),
        out_specs=rows,
        check_vma=False,
    )
```

```python
import functools

import jax
import jax.numpy as jnp
from jax import lax
from jax.experimental import pallas as pl
from jax.experimental.pallas import tpu as pltpu
from jax.sharding import PartitionSpec as P

HEAD_DIM = 64
GROUPS = 4
LANES = 128
MARK = 100.0
MARK_TEST = 64.0
SAFE = 64.0
LOW = -1e30
ONES = 16
MOST_QUERIES = 1024
MOST_KEYS = 2048
LIMIT = 1e30
BF16 = jnp.bfloat16
F32 = jnp.float32
VMEM = pl.BlockSpec(memory_space=pltpu.VMEM)
NT = (((1,), (1,)), ((), ()))
TN = (((0,), (0,)), ((), ()))


MIB = 1024 * 1024


def params(mib=32):
    return pltpu.CompilerParams(vmem_limit_bytes=mib * MIB)


def lower_lanes(shape):
    return lax.broadcasted_iota(jnp.int32, shape, 1) < HEAD_DIM


def swap_halves(x):
    return pltpu.roll(x, HEAD_DIM, 1)


def pack_kernel(rest, per_group, q_hbm, k_hbm, v_hbm, valid_hbm, *refs):
    outs, (q_ref, k_ref, v_ref, valid_ref, sems) = refs[:GROUPS], refs[GROUPS:]
    copies = [
        pltpu.make_async_copy(src, dst, sems.at[i])
        for i, (src, dst) in enumerate(
            ((valid_hbm, valid_ref), (k_hbm, k_ref), (v_hbm, v_ref), (q_hbm, q_ref))
        )
    ]
    for copy in copies:
        copy.start()
    mine = lax.axis_index("inner") // rest
    rows = q_ref.shape[0]
    half = rows // 2
    for copy in copies:
        copy.wait()
    square = (rows, rows)
    on_diagonal = lax.broadcasted_iota(jnp.int32, square, 0) == lax.broadcasted_iota(
        jnp.int32, square, 1
    )
    flag_row = jnp.broadcast_to(valid_ref[...].astype(F32), square)
    picked = jnp.where(on_diagonal, flag_row, 0.0).astype(BF16)
    flags = jnp.dot(picked, jnp.ones((rows, LANES), BF16), preferred_element_type=F32) > 0.5
    low = lower_lanes((rows, LANES))
    low_half = lower_lanes((half, LANES))
    kv_groups, q_groups = [], []
    for g in range(GROUPS):
        kv_slots, q_slots = [], []
        for j in range(per_group):
            h = g * per_group + j
            tile = pl.ds((h // 2) * LANES, LANES)
            k = k_ref[:, tile].astype(F32)
            v = v_ref[:, tile].astype(F32)
            q = q_ref[:, tile].astype(F32) * (HEAD_DIM**-0.5)
            if h % 2 == 0:
                kv = jnp.where(low, k, swap_halves(v))
                qq = jnp.where(low_half, q[:half], swap_halves(q[half:]))
            else:
                kv = jnp.where(low, swap_halves(k), v)
                qq = jnp.where(low_half, swap_halves(q[:half]), q[half:])
            kv_slots.append(jnp.where(flags, kv, MARK))
            q_slots.append(qq)
        kv_groups.append(kv_slots)
        q_groups.append(q_slots)
    for s in range(GROUPS):
        want = jnp.bitwise_xor(mine, s)
        for j in range(per_group):
            lanes = pl.ds(j * LANES, LANES)
            for groups, start, n in ((kv_groups, 0, rows), (q_groups, rows, half)):
                x = groups[0][j]
                for g in range(1, GROUPS):
                    x = jnp.where(want == g, groups[g][j], x)
                outs[s][pl.ds(start, n), lanes] = x.astype(BF16)


def pack(q, k, v, valid, rest):
    rows, width = q.shape
    per_group = width // HEAD_DIM // GROUPS
    slots = per_group * LANES
    return pl.pallas_call(
        functools.partial(pack_kernel, rest, per_group),
        out_shape=[jax.ShapeDtypeStruct((rows + rows // 2, slots), BF16)] * GROUPS,
        in_specs=[pl.BlockSpec(memory_space=pltpu.HBM)] * 4,
        out_specs=[VMEM] * GROUPS,
        scratch_shapes=[pltpu.VMEM((rows, width), BF16)] * 3
        + [pltpu.VMEM((1, rows), jnp.int32), pltpu.SemaphoreType.DMA((4,))],
        compiler_params=params(24),
    )(*[pltpu.with_memory_space_constraint(x, pltpu.HBM) for x in (q, k, v, valid.reshape(1, rows))])


def spread_queries(refs, half, qs):
    start = 0
    for ref in refs:
        for piece in range(ref.shape[0] // half):
            for j in range(qs.shape[1] // LANES):
                lanes = pl.ds(j * LANES, LANES)
                x = ref[pl.ds(piece * half, half), lanes].astype(F32)
                low = lower_lanes(x.shape)
                qs[pl.ds(start, half), lanes] = jnp.where(low, x, 0.0).astype(BF16)
                qs[pl.ds(start + half, half), lanes] = jnp.where(low, swap_halves(x), 0.0).astype(BF16)
            start += 2 * half


def spread_keys(refs, ks, vs):
    start = 0
    for ref in refs:
        n = ref.shape[0]
        for j in range(ks.shape[1] // LANES):
            lanes = pl.ds(j * LANES, LANES)
            x = ref[:, lanes]
            hole = x > jnp.asarray(MARK_TEST, BF16)
            low = lower_lanes(x.shape)
            zero = jnp.zeros_like(x)
            x = jnp.where(hole, zero, x)
            ks[pl.ds(start, n), lanes] = x
            vs[pl.ds(start, n), lanes] = jnp.where(low, jnp.where(hole, zero, jnp.ones_like(x)), x)
        start += n


def largest_norm(ref):
    pick = lower_lanes((16, LANES)).astype(BF16)
    best = None
    for j in range(ref.shape[1] // LANES):
        x = ref[:, pl.ds(j * LANES, LANES)]
        norms = lax.dot_general(pick, x * x, NT, preferred_element_type=F32)
        best = norms if best is None else jnp.maximum(best, norms)
    return jnp.max(best[:8])


def add_keys(work, ks, vs, safe):
    slots = ks.shape[1] // LANES
    rows_k = ks.shape[0]

    @pl.when(safe)
    def _():
        steps = []
        for first_key, fresh, qs, acc, unused in work:
            for j in range(slots):
                for col in range(0, qs.shape[0], MOST_QUERIES):
                    at = pl.ds(col, min(MOST_QUERIES, qs.shape[0] - col))
                    for row in range(first_key, rows_k, MOST_KEYS):
                        ka = pl.ds(row, min(MOST_KEYS, rows_k - row))
                        steps.append((qs, acc, pl.ds(j * LANES, LANES), at, ka, fresh and row == first_key))

        def scores(step):
            qs, unused, lanes, at, ka, unused = step
            return lax.dot_general(ks[ka, lanes], qs[at, lanes], NT, preferred_element_type=F32)

        ahead = scores(steps[0])
        for i, (qs, acc, lanes, at, ka, zero) in enumerate(steps):
            p = jnp.exp(ahead).astype(BF16)
            if i + 1 < len(steps):
                ahead = scores(steps[i + 1])
            term = lax.dot_general(vs[ka, lanes], p, TN, preferred_element_type=F32)
            acc[lanes, at] = term if zero else acc[lanes, at] + term

    @pl.when(jnp.logical_not(safe))
    def _():
        for first_key, fresh, qs, acc, top in work:
            if fresh:
                acc[...] = jnp.zeros_like(acc)
            add_keys_shifted(first_key, qs, ks, vs, acc, top)


def add_keys_shifted(first_key, qs, ks, vs, acc, top):
    slots = ks.shape[1] // LANES
    rows_k = ks.shape[0]
    cols = qs.shape[0]
    step_q, step_k = 128, 128

    def over_queries(i, unused):
        at = pl.ds(pl.multiple_of(i * step_q, step_q), step_q)
        for j in range(slots):
            lanes = pl.ds(j * LANES, LANES)

            def over_keys(c, carry):
                high, total = carry
                ka = pl.ds(pl.multiple_of(c * step_k, step_k), step_k)
                v = vs[ka, lanes]
                s = lax.dot_general(ks[ka, lanes], qs[at, lanes], NT, preferred_element_type=F32)
                s = jnp.where(v[:, :1].astype(F32) > 0.5, s, LOW)
                best = jnp.max(s, axis=0, keepdims=True)
                best = (best + jnp.abs(best) * (1.0 / 128)).astype(BF16).astype(F32)
                new = jnp.maximum(high, best)
                p = jnp.exp(s - new).astype(BF16)
                total = total * jnp.exp(high - new) + lax.dot_general(v, p, TN, preferred_element_type=F32)
                return new, total

            high, total = lax.fori_loop(first_key // step_k, rows_k // step_k, over_keys, (top[pl.ds(j, 1), at], acc[lanes, at]))
            acc[lanes, at] = total
            top[pl.ds(j, 1), at] = high
        return unused

    lax.fori_loop(0, cols // step_q, over_queries, 0)


def attend_kernel(sets, n_kv, half, first, n_export, *refs):
    given = []
    for n_q, unused in sets:
        count = n_q or 3
        given.append(refs[:count])
        refs = refs[count:]
    kv_refs, refs = refs[:n_kv], refs[n_kv:]
    if not first:
        info_in, refs = refs[0], refs[1:]
    held = []
    for (n_q, unused), mine in zip(sets, given):
        count = 3 if n_q else 2
        held.append(refs[:3] if n_q else (mine[0], *refs[:2]))
        refs = refs[count:]
    info, exports, (ks, vs) = refs[0], refs[1 : 1 + n_export], refs[1 + n_export :]
    length = None if first else info_in[...][0, 0]
    for (n_q, unused), mine, (qs, acc, top) in zip(sets, given, held):
        if n_q:
            spread_queries(mine, half, qs)
            top[...] = jnp.zeros_like(top)
            own = largest_norm(qs)
            length = own if length is None else jnp.maximum(length, own)
    spread_keys(kv_refs, ks, vs)
    safe = length * largest_norm(ks) * 1.05 <= SAFE * SAFE
    info[...] = jnp.full(info.shape, jnp.where(safe, length, LIMIT), F32)
    add_keys([(first_key, n_q > 0, *mine) for (n_q, first_key), mine in zip(sets, held)], ks, vs, safe)
    for i, out in enumerate(exports):
        place = 0
        for qs, acc, top in held:
            cols = qs.shape[0] // (n_export + 1)
            at, to = pl.ds((i + 1) * cols, cols), pl.ds(place, cols)
            for j in range(qs.shape[1] // LANES):
                start = j * (HEAD_DIM + 2 * ONES)
                out[pl.ds(start, HEAD_DIM), to] = acc[pl.ds(j * LANES + HEAD_DIM, HEAD_DIM), at].astype(BF16)
                out[pl.ds(start + HEAD_DIM, ONES), to] = acc[pl.ds(j * LANES, ONES), at].astype(BF16)
                shift = jnp.broadcast_to(top[pl.ds(j, 1), at], (ONES, cols))
                out[pl.ds(start + HEAD_DIM + ONES, ONES), to] = shift.astype(BF16)
            place += cols


def attend(sets, kv_list, half, info, n_export=0):
    width = kv_list[0].shape[1]
    slots = width // LANES
    first = info is None
    rows_k = sum(k.shape[0] for k in kv_list)
    args, meta, out_shape, aliases, work, own_cols = [], [], [], {}, 0, 0
    for items, first_key in sets:
        new = items[0].dtype == items[1].dtype
        cols = sum(q.shape[0] for q in items) * 2 if new else items[0].shape[0]
        meta.append((len(items) if new else 0, first_key))
        if new:
            out_shape.append(jax.ShapeDtypeStruct((cols, width), BF16))
        else:
            aliases[len(args) + 1], aliases[len(args) + 2] = len(out_shape), len(out_shape) + 1
        out_shape += [jax.ShapeDtypeStruct((width, cols), F32), jax.ShapeDtypeStruct((8, cols), F32)]
        args += items
        work += cols * (rows_k - first_key)
        own_cols += cols // (n_export + 1)
    args += kv_list
    if not first:
        args.append(info)
    out_shape.append(jax.ShapeDtypeStruct((8, LANES), F32))
    out_shape += [jax.ShapeDtypeStruct((slots * (HEAD_DIM + 2 * ONES), own_cols), BF16)] * n_export
    out = list(
        pl.pallas_call(
            functools.partial(attend_kernel, meta, len(kv_list), half, first, n_export),
            out_shape=out_shape,
            in_specs=[VMEM] * len(args),
            out_specs=[VMEM] * len(out_shape),
            scratch_shapes=[pltpu.VMEM((rows_k, width), BF16)] * 2,
            input_output_aliases=aliases,
            compiler_params=params(),
            cost_estimate=pl.CostEstimate(flops=1, bytes_accessed=1, transcendentals=0),
        )(*args)
    )
    states = []
    for (items, unused), (n_q, unused) in zip(sets, meta):
        states.append([out.pop(0) if n_q else items[0], out.pop(0), out.pop(0)])
    return states, out[0], out[1:]


def finish_kernel(n_sets, n_import, wanted, *refs):
    held = [refs[2 * i : 2 * i + 2] for i in range(n_sets)]
    imports, outs = refs[2 * n_sets : 2 * n_sets + n_import], list(refs[2 * n_sets + n_import :])
    piece = outs[0].shape[1]
    step = HEAD_DIM + 2 * ONES
    place = 0
    for acc, top in held:
        cols = acc.shape[1] // (n_import + 1)
        for col in range(0, cols, piece):
            if (place + col) // piece not in wanted:
                continue
            out = outs.pop(0)
            at, there = pl.ds(col, piece), pl.ds(place + col, piece)
            for j in range(acc.shape[0] // LANES):
                total = acc[pl.ds(j * LANES + HEAD_DIM, HEAD_DIM), at]
                count = acc[pl.ds(j * LANES, 1), at]
                high = top[pl.ds(j, 1), at]
                for ref in imports:
                    values = ref[pl.ds(j * step, HEAD_DIM), there].astype(F32)
                    sums = ref[pl.ds(j * step + HEAD_DIM, ONES), there].astype(F32)[:1]
                    shift = ref[pl.ds(j * step + HEAD_DIM + ONES, ONES), there].astype(F32)[:1]
                    new = jnp.maximum(high, shift)
                    mine, theirs = jnp.exp(high - new), jnp.exp(shift - new)
                    total = total * mine + values * theirs
                    count = count * mine + sums * theirs
                    high = new
                share = 1.0 / (count + jnp.exp(-high))
                out[pl.ds(j * HEAD_DIM, HEAD_DIM), :] = (total * share).astype(BF16)
        place += cols


def finish(states, imports, n_pieces, wanted):
    sums = [x for state in states for x in state[1:]]
    slots = sums[0].shape[0] // LANES
    piece = sum(state[1].shape[1] for state in states) // (len(imports) + 1) // n_pieces
    return pl.pallas_call(
        functools.partial(finish_kernel, len(states), len(imports), wanted),
        out_shape=[jax.ShapeDtypeStruct((slots * HEAD_DIM, piece), BF16)] * len(wanted),
        in_specs=[VMEM] * (len(sums) + len(imports)),
        out_specs=[VMEM] * len(wanted),
        compiler_params=params(),
    )(*sums, *imports)


def project_kernel(rest, *refs):
    parts, w_ref, out = refs[:GROUPS], refs[GROUPS], refs[GROUPS + 1]
    mine = lax.axis_index("inner") // rest
    rows = parts[0].shape[0]
    total = None
    for s, part in enumerate(parts):
        g = jnp.bitwise_xor(mine, s)
        w = w_ref[pl.ds(pl.multiple_of(g * rows, 16), rows), :]
        term = lax.dot_general(part[...], w, TN, preferred_element_type=F32)
        total = term if total is None else total + term
    out[...] = total.astype(BF16)


def project(parts, w, rest):
    return pl.pallas_call(
        functools.partial(project_kernel, rest),
        out_shape=jax.ShapeDtypeStruct((parts[0].shape[1], w.shape[1]), BF16),
        in_specs=[VMEM] * (GROUPS + 1),
        out_specs=VMEM,
        compiler_params=params(),
    )(*parts, w)


def on_device(n_blk, n_inner, q, k, v, valid, w):
    rest = n_inner // GROUPS
    half = q.shape[0] // 2

    def over_groups(x, s):
        return lax.ppermute(x, "inner", [(i, (i // rest ^ s) * rest + i % rest) for i in range(n_inner)])

    def over_rest(x, t):
        return lax.ppermute(x, "inner", [(i, i // rest * rest + (i + t) % rest) for i in range(n_inner)])

    def over_blk(x, t):
        return lax.ppermute(x, "blk", [(i, (i + t) % n_blk) for i in range(n_blk)])

    def plane(chunk, order=(1, 2, 3)):
        return [lax.ppermute(chunk, "blk", [(b, b ^ d) for b in range(n_blk)]) for d in order]

    def after(x, *done):
        return lax.optimization_barrier((x, *done))[0]

    pieces = list(pack(q, k, v, valid, rest))
    rows = q.shape[0]

    def gathered_queries(pieces):
        own = jnp.concatenate([x[rows:] for x in pieces], axis=0)
        return [own] + [over_rest(own, t) for t in range(1, rest)]

    if n_blk == 4 and rest == 2:
        own0 = pieces[0][:rows]
        near0 = plane(own0, (3, 2, 1))
        pieces[1], pieces[2] = over_groups(pieces[1], 1), over_groups(pieces[2], 2)
        pieces[3] = over_groups(after(pieces[3], pieces[1], pieces[2]), 3)
        pieces[1], pieces[2] = after((pieces[1], pieces[2]), *near0)
        q_early = gathered_queries(pieces[:3])
        own1 = after(jnp.concatenate([x[:rows] for x in pieces[1:3]], axis=0), *q_early)
        near1 = plane(own1, (1, 2, 3))
        early = [own0, own1, *near0]
        (early_set,), info, unused = attend([(q_early, 0)], early, half, None)
        last = after(pieces[3], early_set[1])
        own2 = last[:rows]
        near2 = plane(own2, (3, 2, 1))
        q_late = gathered_queries([last])
        met = sum(x.shape[0] for x in early)
        states, info, unused = attend([(early_set, met), (q_late, 0)], [*early, own2], half, info)
        near1 = after(tuple(near1), states[0][1])
        states, info, unused = attend([(x, 0) for x in states], list(near1), half, info)
        states, info, exports = attend([(x, 0) for x in states], near2, half, info, rest - 1)
    else:
        pieces = [pieces[0]] + [over_groups(pieces[s], s) for s in range(1, GROUPS)]
        chunk = jnp.concatenate([x[:rows] for x in pieces], axis=0)
        blocks = [chunk] + [over_blk(chunk, t) for t in range(1, n_blk)]
        states, info, exports = attend([(gathered_queries(pieces), 0)], blocks, half, None, rest - 1)
    imports = [over_rest(x, rest - 1 - t) for t, x in enumerate(exports)]
    there = [over_groups(x, s) for s, x in zip((2, 3), finish(states, imports, GROUPS, (2, 3)))]
    own, beside = finish(states, imports, GROUPS, (0, 1))
    parts = [own, over_groups(beside, 1), *there]
    return project(parts, w, rest)


def solution(mesh):
    rows = P(("blk", "inner"), None)
    return jax.shard_map(
        functools.partial(on_device, mesh.shape["blk"], mesh.shape["inner"]),
        mesh=mesh,
        in_specs=(rows, rows, rows, P(("blk", "inner")), P()),
        out_specs=rows,
        check_vma=False,
    )
```

```python
import functools

import jax
import jax.numpy as jnp
from jax import lax
from jax.experimental import pallas as pl
from jax.experimental.pallas import tpu as pltpu
from jax.sharding import PartitionSpec as P

HEAD_DIM = 64
GROUPS = 4
LANES = 128
MARK = 100.0
MARK_TEST = 64.0
SAFE = 64.0
LOW = -1e30
ONES = 16
MOST_QUERIES = 1024
MOST_KEYS = 2048
LIMIT = 1e30
BF16 = jnp.bfloat16
F32 = jnp.float32
VMEM = pl.BlockSpec(memory_space=pltpu.VMEM)
NT = (((1,), (1,)), ((), ()))
TN = (((0,), (0,)), ((), ()))


MIB = 1024 * 1024


def params(mib=32):
    return pltpu.CompilerParams(vmem_limit_bytes=mib * MIB)


def lower_lanes(shape):
    return lax.broadcasted_iota(jnp.int32, shape, 1) < HEAD_DIM


def swap_halves(x):
    return pltpu.roll(x, HEAD_DIM, 1)


def pack_kernel(rest, per_group, q_hbm, k_hbm, v_hbm, valid_hbm, *refs):
    outs, (q_ref, k_ref, v_ref, valid_ref, sems) = refs[:GROUPS], refs[GROUPS:]
    copies = [
        pltpu.make_async_copy(src, dst, sems.at[i])
        for i, (src, dst) in enumerate(
            ((valid_hbm, valid_ref), (k_hbm, k_ref), (v_hbm, v_ref), (q_hbm, q_ref))
        )
    ]
    for copy in copies:
        copy.start()
    mine = lax.axis_index("inner") // rest
    rows = q_ref.shape[0]
    half = rows // 2
    for copy in copies:
        copy.wait()
    square = (rows, rows)
    on_diagonal = lax.broadcasted_iota(jnp.int32, square, 0) == lax.broadcasted_iota(
        jnp.int32, square, 1
    )
    flag_row = jnp.broadcast_to(valid_ref[...].astype(F32), square)
    picked = jnp.where(on_diagonal, flag_row, 0.0).astype(BF16)
    flags = jnp.dot(picked, jnp.ones((rows, LANES), BF16), preferred_element_type=F32) > 0.5
    low = lower_lanes((rows, LANES))
    low_half = lower_lanes((half, LANES))
    kv_groups, q_groups = [], []
    for g in range(GROUPS):
        kv_slots, q_slots = [], []
        for j in range(per_group):
            h = g * per_group + j
            tile = pl.ds((h // 2) * LANES, LANES)
            k = k_ref[:, tile].astype(F32)
            v = v_ref[:, tile].astype(F32)
            q = q_ref[:, tile].astype(F32) * (HEAD_DIM**-0.5)
            if h % 2 == 0:
                kv = jnp.where(low, k, swap_halves(v))
                qq = jnp.where(low_half, q[:half], swap_halves(q[half:]))
            else:
                kv = jnp.where(low, swap_halves(k), v)
                qq = jnp.where(low_half, swap_halves(q[:half]), q[half:])
            kv_slots.append(jnp.where(flags, kv, MARK))
            q_slots.append(qq)
        kv_groups.append(kv_slots)
        q_groups.append(q_slots)
    for s in range(GROUPS):
        want = jnp.bitwise_xor(mine, s)
        for j in range(per_group):
            lanes = pl.ds(j * LANES, LANES)
            for groups, start, n in ((kv_groups, 0, rows), (q_groups, rows, half)):
                x = groups[0][j]
                for g in range(1, GROUPS):
                    x = jnp.where(want == g, groups[g][j], x)
                outs[s][pl.ds(start, n), lanes] = x.astype(BF16)


def pack(q, k, v, valid, rest):
    rows, width = q.shape
    per_group = width // HEAD_DIM // GROUPS
    slots = per_group * LANES
    return pl.pallas_call(
        functools.partial(pack_kernel, rest, per_group),
        out_shape=[jax.ShapeDtypeStruct((rows + rows // 2, slots), BF16)] * GROUPS,
        in_specs=[pl.BlockSpec(memory_space=pltpu.HBM)] * 4,
        out_specs=[VMEM] * GROUPS,
        scratch_shapes=[pltpu.VMEM((rows, width), BF16)] * 3
        + [pltpu.VMEM((1, rows), jnp.int32), pltpu.SemaphoreType.DMA((4,))],
        compiler_params=params(24),
    )(*[pltpu.with_memory_space_constraint(x, pltpu.HBM) for x in (q, k, v, valid.reshape(1, rows))])


def spread_queries(refs, half, qs):
    start = 0
    for ref in refs:
        for piece in range(ref.shape[0] // half):
            for j in range(qs.shape[1] // LANES):
                lanes = pl.ds(j * LANES, LANES)
                x = ref[pl.ds(piece * half, half), lanes].astype(F32)
                low = lower_lanes(x.shape)
                qs[pl.ds(start, half), lanes] = jnp.where(low, x, 0.0).astype(BF16)
                qs[pl.ds(start + half, half), lanes] = jnp.where(low, swap_halves(x), 0.0).astype(BF16)
            start += 2 * half


def spread_keys(refs, ks, vs):
    start = 0
    for ref in refs:
        n = ref.shape[0]
        for j in range(ks.shape[1] // LANES):
            lanes = pl.ds(j * LANES, LANES)
            x = ref[:, lanes]
            hole = x > jnp.asarray(MARK_TEST, BF16)
            low = lower_lanes(x.shape)
            zero = jnp.zeros_like(x)
            x = jnp.where(hole, zero, x)
            ks[pl.ds(start, n), lanes] = x
            vs[pl.ds(start, n), lanes] = jnp.where(low, jnp.where(hole, zero, jnp.ones_like(x)), x)
        start += n


def largest_norm(ref):
    pick = lower_lanes((16, LANES)).astype(BF16)
    best = None
    for j in range(ref.shape[1] // LANES):
        x = ref[:, pl.ds(j * LANES, LANES)]
        norms = lax.dot_general(pick, x * x, NT, preferred_element_type=F32)
        best = norms if best is None else jnp.maximum(best, norms)
    return jnp.max(best[:8])


def add_keys(work, ks, vs, safe):
    slots = ks.shape[1] // LANES
    rows_k = ks.shape[0]
    steps = []
    for first_key, qs, old_acc, old_top, acc, top in work:
        top[...] = jnp.zeros_like(top) if old_top is None else old_top[...]
        for j in range(slots):
            for col in range(0, qs.shape[0], MOST_QUERIES):
                at = pl.ds(col, min(MOST_QUERIES, qs.shape[0] - col))
                for row in range(first_key, rows_k, MOST_KEYS):
                    ka = pl.ds(row, min(MOST_KEYS, rows_k - row))
                    steps.append((qs, old_acc if row == first_key else acc, acc, pl.ds(j * LANES, LANES), at, ka))

    def scores(step):
        qs, unused, unused, lanes, at, ka = step
        return lax.dot_general(ks[ka, lanes], qs[at, lanes], NT, preferred_element_type=F32)

    ahead = scores(steps[0])
    for i, (qs, base, acc, lanes, at, ka) in enumerate(steps):
        p = jnp.exp(ahead).astype(BF16)
        if i + 1 < len(steps):
            ahead = scores(steps[i + 1])
        term = lax.dot_general(vs[ka, lanes], p, TN, preferred_element_type=F32)
        acc[lanes, at] = term if base is None else base[lanes, at] + term

    @pl.when(jnp.logical_not(safe))
    def _():
        for first_key, qs, old_acc, unused, acc, top in work:
            acc[...] = jnp.zeros_like(acc) if old_acc is None else old_acc[...]
            add_keys_shifted(first_key, qs, ks, vs, acc, top)


def add_keys_shifted(first_key, qs, ks, vs, acc, top):
    slots = ks.shape[1] // LANES
    rows_k = ks.shape[0]
    cols = qs.shape[0]
    step_q, step_k = 128, 128

    def over_queries(i, unused):
        at = pl.ds(pl.multiple_of(i * step_q, step_q), step_q)
        for j in range(slots):
            lanes = pl.ds(j * LANES, LANES)

            def over_keys(c, carry):
                high, total = carry
                ka = pl.ds(pl.multiple_of(c * step_k, step_k), step_k)
                v = vs[ka, lanes]
                s = lax.dot_general(ks[ka, lanes], qs[at, lanes], NT, preferred_element_type=F32)
                s = jnp.where(v[:, :1].astype(F32) > 0.5, s, LOW)
                best = jnp.max(s, axis=0, keepdims=True)
                best = (best + jnp.abs(best) * (1.0 / 128)).astype(BF16).astype(F32)
                new = jnp.maximum(high, best)
                p = jnp.exp(s - new).astype(BF16)
                total = total * jnp.exp(high - new) + lax.dot_general(v, p, TN, preferred_element_type=F32)
                return new, total

            high, total = lax.fori_loop(first_key // step_k, rows_k // step_k, over_keys, (top[pl.ds(j, 1), at], acc[lanes, at]))
            acc[lanes, at] = total
            top[pl.ds(j, 1), at] = high
        return unused

    lax.fori_loop(0, cols // step_q, over_queries, 0)


def attend_kernel(sets, n_kv, half, first, n_export, *refs):
    given = []
    for n_q, unused in sets:
        count = n_q or 3
        given.append(refs[:count])
        refs = refs[count:]
    kv_refs, refs = refs[:n_kv], refs[n_kv:]
    if not first:
        info_in, refs = refs[0], refs[1:]
    held = []
    for (n_q, unused), mine in zip(sets, given):
        count = 3 if n_q else 2
        held.append(refs[:3] if n_q else (mine[0], *refs[:2]))
        refs = refs[count:]
    info, exports, (ks, vs) = refs[0], refs[1 : 1 + n_export], refs[1 + n_export :]
    length = None if first else info_in[...][0, 0]
    for (n_q, unused), mine, (qs, acc, top) in zip(sets, given, held):
        if n_q:
            spread_queries(mine, half, qs)
            own = largest_norm(qs)
            length = own if length is None else jnp.maximum(length, own)
    spread_keys(kv_refs, ks, vs)
    safe = length * largest_norm(ks) * 1.05 <= SAFE * SAFE
    info[...] = jnp.full(info.shape, jnp.where(safe, length, LIMIT), F32)
    work = []
    for (n_q, first_key), mine, (qs, acc, top) in zip(sets, given, held):
        old_acc, old_top = (None, None) if n_q else mine[1:]
        work.append((first_key, qs, old_acc, old_top, acc, top))
    add_keys(work, ks, vs, safe)
    for i, out in enumerate(exports):
        place = 0
        for qs, acc, top in held:
            cols = qs.shape[0] // (n_export + 1)
            at, to = pl.ds((i + 1) * cols, cols), pl.ds(place, cols)
            for j in range(qs.shape[1] // LANES):
                start = j * (HEAD_DIM + 2 * ONES)
                out[pl.ds(start, HEAD_DIM), to] = acc[pl.ds(j * LANES + HEAD_DIM, HEAD_DIM), at].astype(BF16)
                out[pl.ds(start + HEAD_DIM, ONES), to] = acc[pl.ds(j * LANES, ONES), at].astype(BF16)
                shift = jnp.broadcast_to(top[pl.ds(j, 1), at], (ONES, cols))
                out[pl.ds(start + HEAD_DIM + ONES, ONES), to] = shift.astype(BF16)
            place += cols


def attend(sets, kv_list, half, info, n_export=0):
    width = kv_list[0].shape[1]
    slots = width // LANES
    first = info is None
    rows_k = sum(k.shape[0] for k in kv_list)
    args, meta, out_shape, own_cols = [], [], [], 0
    for items, first_key in sets:
        new = items[0].dtype == items[1].dtype
        cols = sum(q.shape[0] for q in items) * 2 if new else items[0].shape[0]
        meta.append((len(items) if new else 0, first_key))
        if new:
            out_shape.append(jax.ShapeDtypeStruct((cols, width), BF16))
        out_shape += [jax.ShapeDtypeStruct((width, cols), F32), jax.ShapeDtypeStruct((8, cols), F32)]
        args += items
        own_cols += cols // (n_export + 1)
    args += kv_list
    if not first:
        args.append(info)
    out_shape.append(jax.ShapeDtypeStruct((8, LANES), F32))
    out_shape += [jax.ShapeDtypeStruct((slots * (HEAD_DIM + 2 * ONES), own_cols), BF16)] * n_export
    out = list(
        pl.pallas_call(
            functools.partial(attend_kernel, meta, len(kv_list), half, first, n_export),
            out_shape=out_shape,
            in_specs=[VMEM] * len(args),
            out_specs=[VMEM] * len(out_shape),
            scratch_shapes=[pltpu.VMEM((rows_k, width), BF16)] * 2,
            compiler_params=params(),
            cost_estimate=pl.CostEstimate(flops=1, bytes_accessed=1, transcendentals=0),
        )(*args)
    )
    states = []
    for (items, unused), (n_q, unused) in zip(sets, meta):
        states.append([out.pop(0) if n_q else items[0], out.pop(0), out.pop(0)])
    return states, out[0], out[1:]


def finish_kernel(n_sets, n_import, wanted, *refs):
    held = [refs[2 * i : 2 * i + 2] for i in range(n_sets)]
    imports, outs = refs[2 * n_sets : 2 * n_sets + n_import], list(refs[2 * n_sets + n_import :])
    piece = outs[0].shape[1]
    step = HEAD_DIM + 2 * ONES
    place = 0
    for acc, top in held:
        cols = acc.shape[1] // (n_import + 1)
        for col in range(0, cols, piece):
            if (place + col) // piece not in wanted:
                continue
            out = outs.pop(0)
            at, there = pl.ds(col, piece), pl.ds(place + col, piece)
            for j in range(acc.shape[0] // LANES):
                total = acc[pl.ds(j * LANES + HEAD_DIM, HEAD_DIM), at]
                count = acc[pl.ds(j * LANES, 1), at]
                high = top[pl.ds(j, 1), at]
                for ref in imports:
                    values = ref[pl.ds(j * step, HEAD_DIM), there].astype(F32)
                    sums = ref[pl.ds(j * step + HEAD_DIM, ONES), there].astype(F32)[:1]
                    shift = ref[pl.ds(j * step + HEAD_DIM + ONES, ONES), there].astype(F32)[:1]
                    new = jnp.maximum(high, shift)
                    mine, theirs = jnp.exp(high - new), jnp.exp(shift - new)
                    total = total * mine + values * theirs
                    count = count * mine + sums * theirs
                    high = new
                share = 1.0 / (count + jnp.exp(-high))
                out[pl.ds(j * HEAD_DIM, HEAD_DIM), :] = (total * share).astype(BF16)
        place += cols


def finish(states, imports, n_pieces, wanted):
    sums = [x for state in states for x in state[1:]]
    slots = sums[0].shape[0] // LANES
    piece = sum(state[1].shape[1] for state in states) // (len(imports) + 1) // n_pieces
    return pl.pallas_call(
        functools.partial(finish_kernel, len(states), len(imports), wanted),
        out_shape=[jax.ShapeDtypeStruct((slots * HEAD_DIM, piece), BF16)] * len(wanted),
        in_specs=[VMEM] * (len(sums) + len(imports)),
        out_specs=[VMEM] * len(wanted),
        compiler_params=params(),
    )(*sums, *imports)


def project_kernel(rest, *refs):
    parts, w_ref, out = refs[:GROUPS], refs[GROUPS], refs[GROUPS + 1]
    mine = lax.axis_index("inner") // rest
    rows = parts[0].shape[0]
    total = None
    for s, part in enumerate(parts):
        g = jnp.bitwise_xor(mine, s)
        w = w_ref[pl.ds(pl.multiple_of(g * rows, 16), rows), :]
        term = lax.dot_general(part[...], w, TN, preferred_element_type=F32)
        total = term if total is None else total + term
    out[...] = total.astype(BF16)


def project(parts, w, rest):
    return pl.pallas_call(
        functools.partial(project_kernel, rest),
        out_shape=jax.ShapeDtypeStruct((parts[0].shape[1], w.shape[1]), BF16),
        in_specs=[VMEM] * (GROUPS + 1),
        out_specs=VMEM,
        compiler_params=params(),
    )(*parts, w)


def on_device(n_blk, n_inner, q, k, v, valid, w):
    rest = n_inner // GROUPS
    half = q.shape[0] // 2

    def over_groups(x, s):
        return lax.ppermute(x, "inner", [(i, (i // rest ^ s) * rest + i % rest) for i in range(n_inner)])

    def over_rest(x, t):
        return lax.ppermute(x, "inner", [(i, i // rest * rest + (i + t) % rest) for i in range(n_inner)])

    def over_blk(x, t):
        return lax.ppermute(x, "blk", [(i, (i + t) % n_blk) for i in range(n_blk)])

    def plane(chunk, order=(1, 2, 3)):
        return [lax.ppermute(chunk, "blk", [(b, b ^ d) for b in range(n_blk)]) for d in order]

    def after(x, *done):
        return lax.optimization_barrier((x, *done))[0]

    pieces = list(pack(q, k, v, valid, rest))
    rows = q.shape[0]

    def gathered_queries(pieces):
        own = jnp.concatenate([x[rows:] for x in pieces], axis=0)
        return [own] + [over_rest(own, t) for t in range(1, rest)]

    if n_blk == 4 and rest == 2:
        own0 = pieces[0][:rows]
        near0 = plane(own0, (3, 2, 1))
        pieces[1], pieces[2] = over_groups(pieces[1], 1), over_groups(pieces[2], 2)
        pieces[3] = over_groups(after(pieces[3], pieces[1], pieces[2]), 3)
        pieces[1], pieces[2] = after((pieces[1], pieces[2]), *near0)
        q_early = gathered_queries(pieces[:3])
        own1 = after(jnp.concatenate([x[:rows] for x in pieces[1:3]], axis=0), *q_early)
        near1 = plane(own1, (1, 2, 3))
        early = [own0, own1, *near0]
        (early_set,), info, unused = attend([(q_early, 0)], early, half, None)
        last = after(pieces[3], early_set[1])
        own2 = last[:rows]
        near2 = plane(own2, (3, 2, 1))
        q_late = gathered_queries([last])
        met = sum(x.shape[0] for x in early)
        states, info, unused = attend([(early_set, met), (q_late, 0)], [*early, own2], half, info)
        near1 = after(tuple(near1), states[0][1])
        states, info, unused = attend([(x, 0) for x in states], list(near1), half, info)
        states, info, exports = attend([(x, 0) for x in states], near2, half, info, rest - 1)
    else:
        pieces = [pieces[0]] + [over_groups(pieces[s], s) for s in range(1, GROUPS)]
        chunk = jnp.concatenate([x[:rows] for x in pieces], axis=0)
        blocks = [chunk] + [over_blk(chunk, t) for t in range(1, n_blk)]
        states, info, exports = attend([(gathered_queries(pieces), 0)], blocks, half, None, rest - 1)
    imports = [over_rest(x, rest - 1 - t) for t, x in enumerate(exports)]
    there = [over_groups(x, s) for s, x in zip((2, 3), finish(states, imports, GROUPS, (2, 3)))]
    own, beside = finish(states, imports, GROUPS, (0, 1))
    parts = [own, over_groups(beside, 1), *there]
    return project(parts, w, rest)


def solution(mesh):
    rows = P(("blk", "inner"), None)
    return jax.shard_map(
        functools.partial(on_device, mesh.shape["blk"], mesh.shape["inner"]),
        mesh=mesh,
        in_specs=(rows, rows, rows, P(("blk", "inner")), P()),
        out_specs=rows,
        check_vma=False,
    )
```

```python
import functools

import jax
import jax.numpy as jnp
from jax import lax
from jax.experimental import pallas as pl
from jax.experimental.pallas import tpu as pltpu
from jax.sharding import PartitionSpec as P

HEAD_DIM = 64
GROUPS = 4
LANES = 128
MARK = 100.0
MARK_TEST = 64.0
SAFE = 64.0
LOW = -1e30
ONES = 16
MOST_QUERIES = 1024
MOST_KEYS = 2048
LIMIT = 1e30
BF16 = jnp.bfloat16
F32 = jnp.float32
VMEM = pl.BlockSpec(memory_space=pltpu.VMEM)
NT = (((1,), (1,)), ((), ()))
TN = (((0,), (0,)), ((), ()))


MIB = 1024 * 1024


def params(mib=32):
    return pltpu.CompilerParams(vmem_limit_bytes=mib * MIB)


def lower_lanes(shape):
    return lax.broadcasted_iota(jnp.int32, shape, 1) < HEAD_DIM


def swap_halves(x):
    return pltpu.roll(x, HEAD_DIM, 1)


def pack_kernel(rest, per_group, q_hbm, k_hbm, v_hbm, valid_hbm, *refs):
    outs, (q_ref, k_ref, v_ref, valid_ref, sems) = refs[:GROUPS], refs[GROUPS:]
    copies = [
        pltpu.make_async_copy(src, dst, sems.at[i])
        for i, (src, dst) in enumerate(
            ((valid_hbm, valid_ref), (k_hbm, k_ref), (v_hbm, v_ref), (q_hbm, q_ref))
        )
    ]
    for copy in copies:
        copy.start()
    mine = lax.axis_index("inner") // rest
    rows = q_ref.shape[0]
    half = rows // 2
    for copy in copies:
        copy.wait()
    square = (rows, rows)
    on_diagonal = lax.broadcasted_iota(jnp.int32, square, 0) == lax.broadcasted_iota(
        jnp.int32, square, 1
    )
    flag_row = jnp.broadcast_to(valid_ref[...].astype(F32), square)
    picked = jnp.where(on_diagonal, flag_row, 0.0).astype(BF16)
    flags = jnp.dot(picked, jnp.ones((rows, LANES), BF16), preferred_element_type=F32) > 0.5
    low = lower_lanes((rows, LANES))
    low_half = lower_lanes((half, LANES))
    kv_groups, q_groups = [], []
    for g in range(GROUPS):
        kv_slots, q_slots = [], []
        for j in range(per_group):
            h = g * per_group + j
            tile = pl.ds((h // 2) * LANES, LANES)
            k = k_ref[:, tile].astype(F32)
            v = v_ref[:, tile].astype(F32)
            q = q_ref[:, tile].astype(F32) * (HEAD_DIM**-0.5)
            if h % 2 == 0:
                kv = jnp.where(low, k, swap_halves(v))
                qq = jnp.where(low_half, q[:half], swap_halves(q[half:]))
            else:
                kv = jnp.where(low, swap_halves(k), v)
                qq = jnp.where(low_half, swap_halves(q[:half]), q[half:])
            kv_slots.append(jnp.where(flags, kv, MARK))
            q_slots.append(qq)
        kv_groups.append(kv_slots)
        q_groups.append(q_slots)
    for s in range(GROUPS):
        want = jnp.bitwise_xor(mine, s)
        for j in range(per_group):
            lanes = pl.ds(j * LANES, LANES)
            for groups, start, n in ((kv_groups, 0, rows), (q_groups, rows, half)):
                x = groups[0][j]
                for g in range(1, GROUPS):
                    x = jnp.where(want == g, groups[g][j], x)
                outs[s][pl.ds(start, n), lanes] = x.astype(BF16)


def pack(q, k, v, valid, rest):
    rows, width = q.shape
    per_group = width // HEAD_DIM // GROUPS
    slots = per_group * LANES
    return pl.pallas_call(
        functools.partial(pack_kernel, rest, per_group),
        out_shape=[jax.ShapeDtypeStruct((rows + rows // 2, slots), BF16)] * GROUPS,
        in_specs=[pl.BlockSpec(memory_space=pltpu.HBM)] * 4,
        out_specs=[VMEM] * GROUPS,
        scratch_shapes=[pltpu.VMEM((rows, width), BF16)] * 3
        + [pltpu.VMEM((1, rows), jnp.int32), pltpu.SemaphoreType.DMA((4,))],
        compiler_params=params(24),
    )(*[pltpu.with_memory_space_constraint(x, pltpu.HBM) for x in (q, k, v, valid.reshape(1, rows))])


def spread_queries(refs, half, qs):
    start = 0
    for ref in refs:
        for piece in range(ref.shape[0] // half):
            for j in range(qs.shape[1] // LANES):
                lanes = pl.ds(j * LANES, LANES)
                x = ref[pl.ds(piece * half, half), lanes].astype(F32)
                low = lower_lanes(x.shape)
                qs[pl.ds(start, half), lanes] = jnp.where(low, x, 0.0).astype(BF16)
                qs[pl.ds(start + half, half), lanes] = jnp.where(low, swap_halves(x), 0.0).astype(BF16)
            start += 2 * half


def spread_keys(refs, ks, vs):
    start = 0
    for ref in refs:
        n = ref.shape[0]
        for j in range(ks.shape[1] // LANES):
            lanes = pl.ds(j * LANES, LANES)
            x = ref[:, lanes]
            hole = x > jnp.asarray(MARK_TEST, BF16)
            low = lower_lanes(x.shape)
            zero = jnp.zeros_like(x)
            x = jnp.where(hole, zero, x)
            ks[pl.ds(start, n), lanes] = x
            vs[pl.ds(start, n), lanes] = jnp.where(low, jnp.where(hole, zero, jnp.ones_like(x)), x)
        start += n


def largest_norm(ref):
    pick = lower_lanes((16, LANES)).astype(BF16)
    best = None
    for j in range(ref.shape[1] // LANES):
        x = ref[:, pl.ds(j * LANES, LANES)]
        norms = lax.dot_general(pick, x * x, NT, preferred_element_type=F32)
        best = norms if best is None else jnp.maximum(best, norms)
    return jnp.max(best[:8])


def add_keys(work, ks, vs, safe):
    slots = ks.shape[1] // LANES
    rows_k = ks.shape[0]
    steps = []
    for first_key, qs, old_acc, old_top, acc, top in work:
        top[...] = jnp.zeros_like(top) if old_top is None else old_top[...]
        for j in range(slots):
            for col in range(0, qs.shape[0], MOST_QUERIES):
                at = pl.ds(col, min(MOST_QUERIES, qs.shape[0] - col))
                for row in range(first_key, rows_k, MOST_KEYS):
                    ka = pl.ds(row, min(MOST_KEYS, rows_k - row))
                    steps.append((qs, old_acc if row == first_key else acc, acc, pl.ds(j * LANES, LANES), at, ka))

    def scores(step):
        qs, unused, unused, lanes, at, ka = step
        return lax.dot_general(ks[ka, lanes], qs[at, lanes], NT, preferred_element_type=F32)

    ahead = scores(steps[0])
    for i, (qs, base, acc, lanes, at, ka) in enumerate(steps):
        p = jnp.exp(ahead).astype(BF16)
        if i + 1 < len(steps):
            ahead = scores(steps[i + 1])
        term = lax.dot_general(vs[ka, lanes], p, TN, preferred_element_type=F32)
        acc[lanes, at] = term if base is None else base[lanes, at] + term

    @pl.when(jnp.logical_not(safe))
    def _():
        for first_key, qs, old_acc, unused, acc, top in work:
            acc[...] = jnp.zeros_like(acc) if old_acc is None else old_acc[...]
            add_keys_shifted(first_key, qs, ks, vs, acc, top)


def add_keys_shifted(first_key, qs, ks, vs, acc, top):
    slots = ks.shape[1] // LANES
    rows_k = ks.shape[0]
    cols = qs.shape[0]
    step_q, step_k = 128, 128

    def over_queries(i, unused):
        at = pl.ds(pl.multiple_of(i * step_q, step_q), step_q)
        for j in range(slots):
            lanes = pl.ds(j * LANES, LANES)

            def over_keys(c, carry):
                high, total = carry
                ka = pl.ds(pl.multiple_of(c * step_k, step_k), step_k)
                v = vs[ka, lanes]
                s = lax.dot_general(ks[ka, lanes], qs[at, lanes], NT, preferred_element_type=F32)
                s = jnp.where(v[:, :1].astype(F32) > 0.5, s, LOW)
                best = jnp.max(s, axis=0, keepdims=True)
                best = (best + jnp.abs(best) * (1.0 / 128)).astype(BF16).astype(F32)
                new = jnp.maximum(high, best)
                p = jnp.exp(s - new).astype(BF16)
                total = total * jnp.exp(high - new) + lax.dot_general(v, p, TN, preferred_element_type=F32)
                return new, total

            high, total = lax.fori_loop(first_key // step_k, rows_k // step_k, over_keys, (top[pl.ds(j, 1), at], acc[lanes, at]))
            acc[lanes, at] = total
            top[pl.ds(j, 1), at] = high
        return unused

    lax.fori_loop(0, cols // step_q, over_queries, 0)


def attend_kernel(sets, n_kv, half, first, n_export, *refs):
    given = []
    for n_q, unused in sets:
        count = n_q or 3
        given.append(refs[:count])
        refs = refs[count:]
    kv_refs, refs = refs[:n_kv], refs[n_kv:]
    if not first:
        info_in, refs = refs[0], refs[1:]
    held = []
    for (n_q, unused), mine in zip(sets, given):
        count = 3 if n_q else 2
        held.append(refs[:3] if n_q else (mine[0], *refs[:2]))
        refs = refs[count:]
    info, exports, (ks, vs) = refs[0], refs[1 : 1 + n_export], refs[1 + n_export :]
    length = None if first else info_in[...][0, 0]
    for (n_q, unused), mine, (qs, acc, top) in zip(sets, given, held):
        if n_q:
            spread_queries(mine, half, qs)
            own = largest_norm(qs)
            length = own if length is None else jnp.maximum(length, own)
    spread_keys(kv_refs, ks, vs)
    safe = jnp.logical_and(length * largest_norm(ks) * 1.05 <= SAFE * SAFE, length < LIMIT)
    info[...] = jnp.full(info.shape, jnp.where(safe, length, LIMIT), F32)
    work = []
    for (n_q, first_key), mine, (qs, acc, top) in zip(sets, given, held):
        old_acc, old_top = (None, None) if n_q else mine[1:]
        work.append((first_key, qs, old_acc, old_top, acc, top))
    add_keys(work, ks, vs, safe)
    for i, out in enumerate(exports):
        place = 0
        for qs, acc, top in held:
            cols = qs.shape[0] // (n_export + 1)
            at, to = pl.ds((i + 1) * cols, cols), pl.ds(place, cols)
            for j in range(qs.shape[1] // LANES):
                start = j * (HEAD_DIM + ONES)
                out[pl.ds(start, HEAD_DIM), to] = acc[pl.ds(j * LANES + HEAD_DIM, HEAD_DIM), at].astype(BF16)
                sums = acc[pl.ds(j * LANES, ONES), at]
                shift = jnp.broadcast_to(top[pl.ds(j, 1), at], sums.shape)
                upper = lax.broadcasted_iota(jnp.int32, sums.shape, 0) < ONES // 2
                out[pl.ds(start + HEAD_DIM, ONES), to] = jnp.where(upper, sums, shift).astype(BF16)
            place += cols


def attend(sets, kv_list, half, info, n_export=0):
    width = kv_list[0].shape[1]
    slots = width // LANES
    first = info is None
    rows_k = sum(k.shape[0] for k in kv_list)
    args, meta, out_shape, own_cols = [], [], [], 0
    for items, first_key in sets:
        new = items[0].dtype == items[1].dtype
        cols = sum(q.shape[0] for q in items) * 2 if new else items[0].shape[0]
        meta.append((len(items) if new else 0, first_key))
        if new:
            out_shape.append(jax.ShapeDtypeStruct((cols, width), BF16))
        out_shape += [jax.ShapeDtypeStruct((width, cols), F32), jax.ShapeDtypeStruct((8, cols), F32)]
        args += items
        own_cols += cols // (n_export + 1)
    args += kv_list
    if not first:
        args.append(info)
    out_shape.append(jax.ShapeDtypeStruct((8, LANES), F32))
    out_shape += [jax.ShapeDtypeStruct((slots * (HEAD_DIM + ONES), own_cols), BF16)] * n_export
    out = list(
        pl.pallas_call(
            functools.partial(attend_kernel, meta, len(kv_list), half, first, n_export),
            out_shape=out_shape,
            in_specs=[VMEM] * len(args),
            out_specs=[VMEM] * len(out_shape),
            scratch_shapes=[pltpu.VMEM((rows_k, width), BF16)] * 2,
            compiler_params=params(),
            cost_estimate=pl.CostEstimate(flops=1, bytes_accessed=1, transcendentals=0),
        )(*args)
    )
    states = []
    for (items, unused), (n_q, unused) in zip(sets, meta):
        states.append([out.pop(0) if n_q else items[0], out.pop(0), out.pop(0)])
    return states, out[0], out[1:]


def finish_kernel(n_sets, n_import, wanted, *refs):
    held = [refs[2 * i : 2 * i + 2] for i in range(n_sets)]
    imports, outs = refs[2 * n_sets : 2 * n_sets + n_import], list(refs[2 * n_sets + n_import :])
    piece = outs[0].shape[1]
    step = HEAD_DIM + ONES
    place = 0
    for acc, top in held:
        cols = acc.shape[1] // (n_import + 1)
        for col in range(0, cols, piece):
            if (place + col) // piece not in wanted:
                continue
            out = outs.pop(0)
            at, there = pl.ds(col, piece), pl.ds(place + col, piece)
            for j in range(acc.shape[0] // LANES):
                total = acc[pl.ds(j * LANES + HEAD_DIM, HEAD_DIM), at]
                count = acc[pl.ds(j * LANES, 1), at]
                high = top[pl.ds(j, 1), at]
                for ref in imports:
                    values = ref[pl.ds(j * step, HEAD_DIM), there].astype(F32)
                    both = ref[pl.ds(j * step + HEAD_DIM, ONES), there].astype(F32)
                    sums, shift = both[:1], both[ONES // 2 : ONES // 2 + 1]
                    new = jnp.maximum(high, shift)
                    mine, theirs = jnp.exp(high - new), jnp.exp(shift - new)
                    total = total * mine + values * theirs
                    count = count * mine + sums * theirs
                    high = new
                share = 1.0 / (count + jnp.exp(-high))
                out[pl.ds(j * HEAD_DIM, HEAD_DIM), :] = (total * share).astype(BF16)
        place += cols


def finish(states, imports, n_pieces, wanted):
    sums = [x for state in states for x in state[1:]]
    slots = sums[0].shape[0] // LANES
    piece = sum(state[1].shape[1] for state in states) // (len(imports) + 1) // n_pieces
    return pl.pallas_call(
        functools.partial(finish_kernel, len(states), len(imports), wanted),
        out_shape=[jax.ShapeDtypeStruct((slots * HEAD_DIM, piece), BF16)] * len(wanted),
        in_specs=[VMEM] * (len(sums) + len(imports)),
        out_specs=[VMEM] * len(wanted),
        compiler_params=params(),
    )(*sums, *imports)


def project_kernel(rest, *refs):
    parts, w_ref, out = refs[:GROUPS], refs[GROUPS], refs[GROUPS + 1]
    mine = lax.axis_index("inner") // rest
    rows = parts[0].shape[0]
    total = None
    for s, part in enumerate(parts):
        g = jnp.bitwise_xor(mine, s)
        w = w_ref[pl.ds(pl.multiple_of(g * rows, 16), rows), :]
        term = lax.dot_general(part[...], w, TN, preferred_element_type=F32)
        total = term if total is None else total + term
    out[...] = total.astype(BF16)


def project(parts, w, rest):
    return pl.pallas_call(
        functools.partial(project_kernel, rest),
        out_shape=jax.ShapeDtypeStruct((parts[0].shape[1], w.shape[1]), BF16),
        in_specs=[VMEM] * (GROUPS + 1),
        out_specs=VMEM,
        compiler_params=params(),
    )(*parts, w)


def on_device(n_blk, n_inner, q, k, v, valid, w):
    rest = n_inner // GROUPS
    half = q.shape[0] // 2

    def over_groups(x, s):
        return lax.ppermute(x, "inner", [(i, (i // rest ^ s) * rest + i % rest) for i in range(n_inner)])

    def over_rest(x, t):
        return lax.ppermute(x, "inner", [(i, i // rest * rest + (i + t) % rest) for i in range(n_inner)])

    def over_blk(x, t):
        return lax.ppermute(x, "blk", [(i, (i + t) % n_blk) for i in range(n_blk)])

    def plane(chunk, order=(1, 2, 3)):
        return [lax.ppermute(chunk, "blk", [(b, b ^ d) for b in range(n_blk)]) for d in order]

    def after(x, *done):
        return lax.optimization_barrier((x, *done))[0]

    pieces = list(pack(q, k, v, valid, rest))
    rows = q.shape[0]

    def gathered_queries(pieces):
        own = jnp.concatenate([x[rows:] for x in pieces], axis=0)
        return [own] + [over_rest(own, t) for t in range(1, rest)]

    if n_blk == 4 and rest == 2:
        own0 = pieces[0][:rows]
        near0 = plane(own0, (3, 2, 1))
        pieces[2], pieces[1] = over_groups(pieces[2], 2), over_groups(pieces[1], 1)
        pieces[3] = over_groups(after(pieces[3], pieces[1], pieces[2]), 3)
        pieces[1], pieces[2] = after((pieces[1], pieces[2]), *near0)
        q_early = gathered_queries(pieces[:3])
        own1 = after(jnp.concatenate([x[:rows] for x in pieces[1:3]], axis=0), *q_early)
        near1 = plane(own1, (1, 2, 3))
        early = [own0, own1, *near0]
        (early_set,), info, unused = attend([(q_early, 0)], early, half, None)
        last = after(pieces[3], early_set[1])
        own2 = last[:rows]
        near2 = plane(own2, (3, 2, 1))
        q_late = gathered_queries([last])
        met = sum(x.shape[0] for x in early)
        states, info, unused = attend([(early_set, met), (q_late, 0)], [*early, own2], half, info)
        near1 = after(tuple(near1), states[0][1])
        states, info, unused = attend([(x, 0) for x in states], list(near1), half, info)
        states, info, exports = attend([(x, 0) for x in states], near2, half, info, rest - 1)
    else:
        pieces = [pieces[0]] + [over_groups(pieces[s], s) for s in range(1, GROUPS)]
        chunk = jnp.concatenate([x[:rows] for x in pieces], axis=0)
        blocks = [chunk] + [over_blk(chunk, t) for t in range(1, n_blk)]
        states, info, exports = attend([(gathered_queries(pieces), 0)], blocks, half, None, rest - 1)
    imports = [over_rest(x, rest - 1 - t) for t, x in enumerate(exports)]
    there = [over_groups(x, s) for s, x in zip((2, 3), finish(states, imports, GROUPS, (2, 3)))]
    own, beside = finish(states, imports, GROUPS, (0, 1))
    parts = [own, over_groups(beside, 1), *there]
    return project(parts, w, rest)


def solution(mesh):
    rows = P(("blk", "inner"), None)
    return jax.shard_map(
        functools.partial(on_device, mesh.shape["blk"], mesh.shape["inner"]),
        mesh=mesh,
        in_specs=(rows, rows, rows, P(("blk", "inner")), P()),
        out_specs=rows,
        check_vma=False,
    )
```

```python
import functools

import jax
import jax.numpy as jnp
from jax import lax
from jax.experimental import pallas as pl
from jax.experimental.pallas import tpu as pltpu
from jax.sharding import PartitionSpec as P

HEAD_DIM = 64
GROUPS = 4
LANES = 128
MARK = 100.0
MARK_TEST = 64.0
SAFE = 64.0
LOW = -1e30
ONES = 16
MOST_QUERIES = 1024
MOST_KEYS = 2048
LIMIT = 1e30
BF16 = jnp.bfloat16
F32 = jnp.float32
VMEM = pl.BlockSpec(memory_space=pltpu.VMEM)
NT = (((1,), (1,)), ((), ()))
TN = (((0,), (0,)), ((), ()))


MIB = 1024 * 1024


def params(mib=32):
    return pltpu.CompilerParams(vmem_limit_bytes=mib * MIB)


def lower_lanes(shape):
    return lax.broadcasted_iota(jnp.int32, shape, 1) < HEAD_DIM


def swap_halves(x):
    return pltpu.roll(x, HEAD_DIM, 1)


def pack_kernel(rest, per_group, q_hbm, k_hbm, v_hbm, valid_hbm, *refs):
    outs, (q_ref, k_ref, v_ref, valid_ref, sems) = refs[:GROUPS], refs[GROUPS:]
    copies = [
        pltpu.make_async_copy(src, dst, sems.at[i])
        for i, (src, dst) in enumerate(
            ((valid_hbm, valid_ref), (k_hbm, k_ref), (v_hbm, v_ref), (q_hbm, q_ref))
        )
    ]
    for copy in copies:
        copy.start()
    mine = lax.axis_index("inner") // rest
    rows = q_ref.shape[0]
    half = rows // 2
    for copy in copies:
        copy.wait()
    square = (rows, rows)
    on_diagonal = lax.broadcasted_iota(jnp.int32, square, 0) == lax.broadcasted_iota(
        jnp.int32, square, 1
    )
    flag_row = jnp.broadcast_to(valid_ref[...].astype(F32), square)
    picked = jnp.where(on_diagonal, flag_row, 0.0).astype(BF16)
    flags = jnp.dot(picked, jnp.ones((rows, LANES), BF16), preferred_element_type=F32) > 0.5
    low = lower_lanes((rows, LANES))
    low_half = lower_lanes((half, LANES))
    kv_groups, q_groups = [], []
    for g in range(GROUPS):
        kv_slots, q_slots = [], []
        for j in range(per_group):
            h = g * per_group + j
            tile = pl.ds((h // 2) * LANES, LANES)
            k = k_ref[:, tile].astype(F32)
            v = v_ref[:, tile].astype(F32)
            q = q_ref[:, tile].astype(F32) * (HEAD_DIM**-0.5)
            if h % 2 == 0:
                kv = jnp.where(low, k, swap_halves(v))
                qq = jnp.where(low_half, q[:half], swap_halves(q[half:]))
            else:
                kv = jnp.where(low, swap_halves(k), v)
                qq = jnp.where(low_half, swap_halves(q[:half]), q[half:])
            kv_slots.append(jnp.where(flags, kv, MARK))
            q_slots.append(qq)
        kv_groups.append(kv_slots)
        q_groups.append(q_slots)
    for s in range(GROUPS):
        want = jnp.bitwise_xor(mine, s)
        for j in range(per_group):
            lanes = pl.ds(j * LANES, LANES)
            for groups, start, n in ((kv_groups, 0, rows), (q_groups, rows, half)):
                x = groups[0][j]
                for g in range(1, GROUPS):
                    x = jnp.where(want == g, groups[g][j], x)
                outs[s][pl.ds(start, n), lanes] = x.astype(BF16)


def pack(q, k, v, valid, rest):
    rows, width = q.shape
    per_group = width // HEAD_DIM // GROUPS
    slots = per_group * LANES
    return pl.pallas_call(
        functools.partial(pack_kernel, rest, per_group),
        out_shape=[jax.ShapeDtypeStruct((rows + rows // 2, slots), BF16)] * GROUPS,
        in_specs=[pl.BlockSpec(memory_space=pltpu.HBM)] * 4,
        out_specs=[VMEM] * GROUPS,
        scratch_shapes=[pltpu.VMEM((rows, width), BF16)] * 3
        + [pltpu.VMEM((1, rows), jnp.int32), pltpu.SemaphoreType.DMA((4,))],
        compiler_params=params(24),
    )(*[pltpu.with_memory_space_constraint(x, pltpu.HBM) for x in (q, k, v, valid.reshape(1, rows))])


def spread_queries(refs, half, qs):
    start = 0
    for ref in refs:
        for piece in range(ref.shape[0] // half):
            for j in range(qs.shape[1] // LANES):
                lanes = pl.ds(j * LANES, LANES)
                x = ref[pl.ds(piece * half, half), lanes].astype(F32)
                low = lower_lanes(x.shape)
                qs[pl.ds(start, half), lanes] = jnp.where(low, x, 0.0).astype(BF16)
                qs[pl.ds(start + half, half), lanes] = jnp.where(low, swap_halves(x), 0.0).astype(BF16)
            start += 2 * half


def spread_keys(refs, ks, vs):
    start = 0
    for ref in refs:
        n = ref.shape[0]
        for j in range(ks.shape[1] // LANES):
            lanes = pl.ds(j * LANES, LANES)
            x = ref[:, lanes]
            hole = x > jnp.asarray(MARK_TEST, BF16)
            low = lower_lanes(x.shape)
            zero = jnp.zeros_like(x)
            x = jnp.where(hole, zero, x)
            ks[pl.ds(start, n), lanes] = x
            vs[pl.ds(start, n), lanes] = jnp.where(low, jnp.where(hole, zero, jnp.ones_like(x)), x)
        start += n


def largest_norm(ref):
    pick = lower_lanes((16, LANES)).astype(BF16)
    best = None
    for j in range(ref.shape[1] // LANES):
        x = ref[:, pl.ds(j * LANES, LANES)]
        norms = lax.dot_general(pick, x * x, NT, preferred_element_type=F32)
        best = norms if best is None else jnp.maximum(best, norms)
    return jnp.max(best[:8])


def add_keys(work, ks, vs, safe):
    slots = ks.shape[1] // LANES
    rows_k = ks.shape[0]
    steps = []
    for first_key, qs, old_acc, old_top, acc, top in work:
        top[...] = jnp.zeros_like(top) if old_top is None else old_top[...]
        for j in range(slots):
            for col in range(0, qs.shape[0], MOST_QUERIES):
                at = pl.ds(col, min(MOST_QUERIES, qs.shape[0] - col))
                for row in range(first_key, rows_k, MOST_KEYS):
                    ka = pl.ds(row, min(MOST_KEYS, rows_k - row))
                    steps.append((qs, old_acc if row == first_key else acc, acc, pl.ds(j * LANES, LANES), at, ka))

    def scores(step):
        qs, unused, unused, lanes, at, ka = step
        return lax.dot_general(ks[ka, lanes], qs[at, lanes], NT, preferred_element_type=F32)

    ahead = scores(steps[0])
    for i, (qs, base, acc, lanes, at, ka) in enumerate(steps):
        p = jnp.exp(ahead).astype(BF16)
        if i + 1 < len(steps):
            ahead = scores(steps[i + 1])
        term = lax.dot_general(vs[ka, lanes], p, TN, preferred_element_type=F32)
        acc[lanes, at] = term if base is None else base[lanes, at] + term

    @pl.when(jnp.logical_not(safe))
    def _():
        for first_key, qs, old_acc, unused, acc, top in work:
            acc[...] = jnp.zeros_like(acc) if old_acc is None else old_acc[...]
            add_keys_shifted(first_key, qs, ks, vs, acc, top)


def add_keys_shifted(first_key, qs, ks, vs, acc, top):
    slots = ks.shape[1] // LANES
    rows_k = ks.shape[0]
    cols = qs.shape[0]
    step_q, step_k = 128, 128

    def over_queries(i, unused):
        at = pl.ds(pl.multiple_of(i * step_q, step_q), step_q)
        for j in range(slots):
            lanes = pl.ds(j * LANES, LANES)

            def over_keys(c, carry):
                high, total = carry
                ka = pl.ds(pl.multiple_of(c * step_k, step_k), step_k)
                v = vs[ka, lanes]
                s = lax.dot_general(ks[ka, lanes], qs[at, lanes], NT, preferred_element_type=F32)
                s = jnp.where(v[:, :1].astype(F32) > 0.5, s, LOW)
                best = jnp.max(s, axis=0, keepdims=True)
                best = (best + jnp.abs(best) * (1.0 / 128)).astype(BF16).astype(F32)
                new = jnp.maximum(high, best)
                p = jnp.exp(s - new).astype(BF16)
                total = total * jnp.exp(high - new) + lax.dot_general(v, p, TN, preferred_element_type=F32)
                return new, total

            high, total = lax.fori_loop(first_key // step_k, rows_k // step_k, over_keys, (top[pl.ds(j, 1), at], acc[lanes, at]))
            acc[lanes, at] = total
            top[pl.ds(j, 1), at] = high
        return unused

    lax.fori_loop(0, cols // step_q, over_queries, 0)


def attend_kernel(sets, n_kv, half, first, n_export, *refs):
    given = []
    for n_q, unused in sets:
        count = n_q or 3
        given.append(refs[:count])
        refs = refs[count:]
    kv_refs, refs = refs[:n_kv], refs[n_kv:]
    if not first:
        info_in, refs = refs[0], refs[1:]
    held = []
    for (n_q, unused), mine in zip(sets, given):
        count = 3 if n_q else 2
        held.append(refs[:3] if n_q else (mine[0], *refs[:2]))
        refs = refs[count:]
    info, exports, (ks, vs) = refs[0], refs[1 : 1 + n_export], refs[1 + n_export :]
    length = None if first else info_in[...][0, 0]
    for (n_q, unused), mine, (qs, acc, top) in zip(sets, given, held):
        if n_q:
            spread_queries(mine, half, qs)
            own = largest_norm(qs)
            length = own if length is None else jnp.maximum(length, own)
    spread_keys(kv_refs, ks, vs)
    safe = jnp.logical_and(length * largest_norm(ks) * 1.05 <= SAFE * SAFE, length < LIMIT)
    info[...] = jnp.full(info.shape, jnp.where(safe, length, LIMIT), F32)
    work = []
    for (n_q, first_key), mine, (qs, acc, top) in zip(sets, given, held):
        old_acc, old_top = (None, None) if n_q else mine[1:]
        work.append((first_key, qs, old_acc, old_top, acc, top))
    add_keys(work, ks, vs, safe)
    for i, out in enumerate(exports):
        place = 0
        for qs, acc, top in held:
            cols = qs.shape[0] // (n_export + 1)
            at, to = pl.ds((i + 1) * cols, cols), pl.ds(place, cols)
            for j in range(qs.shape[1] // LANES):
                start = j * (HEAD_DIM + ONES)
                out[pl.ds(start, HEAD_DIM), to] = acc[pl.ds(j * LANES + HEAD_DIM, HEAD_DIM), at].astype(BF16)
                sums = acc[pl.ds(j * LANES, ONES), at]
                shift = jnp.broadcast_to(top[pl.ds(j, 1), at], sums.shape)
                upper = lax.broadcasted_iota(jnp.int32, sums.shape, 0) < ONES // 2
                out[pl.ds(start + HEAD_DIM, ONES), to] = jnp.where(upper, sums, shift).astype(BF16)
            place += cols


def attend(sets, kv_list, half, info, n_export=0):
    width = kv_list[0].shape[1]
    slots = width // LANES
    first = info is None
    rows_k = sum(k.shape[0] for k in kv_list)
    args, meta, out_shape, own_cols = [], [], [], 0
    for items, first_key in sets:
        new = items[0].dtype == items[1].dtype
        cols = sum(q.shape[0] for q in items) * 2 if new else items[0].shape[0]
        meta.append((len(items) if new else 0, first_key))
        if new:
            out_shape.append(jax.ShapeDtypeStruct((cols, width), BF16))
        out_shape += [jax.ShapeDtypeStruct((width, cols), F32), jax.ShapeDtypeStruct((8, cols), F32)]
        args += items
        own_cols += cols // (n_export + 1)
    args += kv_list
    if not first:
        args.append(info)
    out_shape.append(jax.ShapeDtypeStruct((8, LANES), F32))
    out_shape += [jax.ShapeDtypeStruct((slots * (HEAD_DIM + ONES), own_cols), BF16)] * n_export
    out = list(
        pl.pallas_call(
            functools.partial(attend_kernel, meta, len(kv_list), half, first, n_export),
            out_shape=out_shape,
            in_specs=[VMEM] * len(args),
            out_specs=[VMEM] * len(out_shape),
            scratch_shapes=[pltpu.VMEM((rows_k, width), BF16)] * 2,
            compiler_params=params(),
            cost_estimate=pl.CostEstimate(flops=1, bytes_accessed=1, transcendentals=0),
        )(*args)
    )
    states = []
    for (items, unused), (n_q, unused) in zip(sets, meta):
        states.append([out.pop(0) if n_q else items[0], out.pop(0), out.pop(0)])
    return states, out[0], out[1:]


def finish_kernel(n_sets, n_import, wanted, *refs):
    held = [refs[2 * i : 2 * i + 2] for i in range(n_sets)]
    imports, outs = refs[2 * n_sets : 2 * n_sets + n_import], list(refs[2 * n_sets + n_import :])
    piece = outs[0].shape[1]
    step = HEAD_DIM + ONES
    place = 0
    for acc, top in held:
        cols = acc.shape[1] // (n_import + 1)
        for col in range(0, cols, piece):
            if (place + col) // piece not in wanted:
                continue
            out = outs.pop(0)
            at, there = pl.ds(col, piece), pl.ds(place + col, piece)
            for j in range(acc.shape[0] // LANES):
                total = acc[pl.ds(j * LANES + HEAD_DIM, HEAD_DIM), at]
                count = acc[pl.ds(j * LANES, 1), at]
                high = top[pl.ds(j, 1), at]
                for ref in imports:
                    values = ref[pl.ds(j * step, HEAD_DIM), there].astype(F32)
                    both = ref[pl.ds(j * step + HEAD_DIM, ONES), there].astype(F32)
                    sums, shift = both[:1], both[ONES // 2 : ONES // 2 + 1]
                    new = jnp.maximum(high, shift)
                    mine, theirs = jnp.exp(high - new), jnp.exp(shift - new)
                    total = total * mine + values * theirs
                    count = count * mine + sums * theirs
                    high = new
                share = 1.0 / (count + jnp.exp(-high))
                out[pl.ds(j * HEAD_DIM, HEAD_DIM), :] = (total * share).astype(BF16)
        place += cols


def finish(states, imports, n_pieces, wanted):
    sums = [x for state in states for x in state[1:]]
    slots = sums[0].shape[0] // LANES
    piece = sum(state[1].shape[1] for state in states) // (len(imports) + 1) // n_pieces
    return pl.pallas_call(
        functools.partial(finish_kernel, len(states), len(imports), wanted),
        out_shape=[jax.ShapeDtypeStruct((slots * HEAD_DIM, piece), BF16)] * len(wanted),
        in_specs=[VMEM] * (len(sums) + len(imports)),
        out_specs=[VMEM] * len(wanted),
        compiler_params=params(),
    )(*sums, *imports)


def project_kernel(rest, *refs):
    parts, w_ref, out = refs[:GROUPS], refs[GROUPS], refs[GROUPS + 1]
    mine = lax.axis_index("inner") // rest
    rows = parts[0].shape[0]
    total = None
    for s, part in enumerate(parts):
        g = jnp.bitwise_xor(mine, s)
        w = w_ref[pl.ds(pl.multiple_of(g * rows, 16), rows), :]
        term = lax.dot_general(part[...], w, TN, preferred_element_type=F32)
        total = term if total is None else total + term
    out[...] = total.astype(BF16)


def project(parts, w, rest):
    return pl.pallas_call(
        functools.partial(project_kernel, rest),
        out_shape=jax.ShapeDtypeStruct((parts[0].shape[1], w.shape[1]), BF16),
        in_specs=[VMEM] * (GROUPS + 1),
        out_specs=VMEM,
        compiler_params=params(),
    )(*parts, w)


def on_device(n_blk, n_inner, q, k, v, valid, w):
    rest = n_inner // GROUPS
    half = q.shape[0] // 2

    def over_groups(x, s):
        return lax.ppermute(x, "inner", [(i, (i // rest ^ s) * rest + i % rest) for i in range(n_inner)])

    def over_rest(x, t):
        return lax.ppermute(x, "inner", [(i, i // rest * rest + (i + t) % rest) for i in range(n_inner)])

    def over_blk(x, t):
        return lax.ppermute(x, "blk", [(i, (i + t) % n_blk) for i in range(n_blk)])

    def plane(chunk, order=(1, 2, 3)):
        return [lax.ppermute(chunk, "blk", [(b, b ^ d) for b in range(n_blk)]) for d in order]

    def after(x, *done):
        return lax.optimization_barrier((x, *done))[0]

    pieces = list(pack(q, k, v, valid, rest))
    rows = q.shape[0]

    def gathered_queries(pieces):
        own = jnp.concatenate([x[rows:] for x in pieces], axis=0)
        return [own] + [over_rest(own, t) for t in range(1, rest)]

    if n_blk == 4 and rest == 2:
        own0 = pieces[0][:rows]
        near0 = plane(own0, (3, 2, 1))
        pieces[2], pieces[1] = over_groups(pieces[2], 2), over_groups(pieces[1], 1)
        pieces[3] = over_groups(after(pieces[3], pieces[1], pieces[2]), 3)
        pieces[1], pieces[2] = after((pieces[1], pieces[2]), *near0)
        q_early = gathered_queries(pieces[:3])
        own1 = after(jnp.concatenate([x[:rows] for x in pieces[1:3]], axis=0), *q_early)
        near1 = plane(own1, (1, 2, 3))
        early = [own0, own1, *near0]
        (early_set,), info, unused = attend([(q_early, 0)], early, half, None)
        last = after(pieces[3], early_set[1])
        own2 = last[:rows]
        near2 = plane(own2, (3, 2, 1))
        q_late = gathered_queries([last])
        met = sum(x.shape[0] for x in early)
        states, info, unused = attend([(early_set, met), (q_late, 0)], [*early, own2, near1[2]], half, info)
        near1 = after(tuple(near1[:2]), states[0][1])
        states, info, unused = attend([(x, 0) for x in states], list(near1), half, info)
        states, info, exports = attend([(x, 0) for x in states], near2, half, info, rest - 1)
    else:
        pieces = [pieces[0]] + [over_groups(pieces[s], s) for s in range(1, GROUPS)]
        chunk = jnp.concatenate([x[:rows] for x in pieces], axis=0)
        blocks = [chunk] + [over_blk(chunk, t) for t in range(1, n_blk)]
        states, info, exports = attend([(gathered_queries(pieces), 0)], blocks, half, None, rest - 1)
    imports = [over_rest(x, rest - 1 - t) for t, x in enumerate(exports)]
    there = [over_groups(x, s) for s, x in zip((2, 3), finish(states, imports, GROUPS, (2, 3)))]
    own, beside = finish(states, imports, GROUPS, (0, 1))
    parts = [own, over_groups(beside, 1), *there]
    return project(parts, w, rest)


def solution(mesh):
    rows = P(("blk", "inner"), None)
    return jax.shard_map(
        functools.partial(on_device, mesh.shape["blk"], mesh.shape["inner"]),
        mesh=mesh,
        in_specs=(rows, rows, rows, P(("blk", "inner")), P()),
        out_specs=rows,
        check_vma=False,
    )
```

```python
import functools

import jax
import jax.numpy as jnp
from jax import lax
from jax.experimental import pallas as pl
from jax.experimental.pallas import tpu as pltpu
from jax.sharding import PartitionSpec as P

HEAD_DIM = 64
GROUPS = 4
LANES = 128
MARK = 100.0
MARK_TEST = 64.0
SAFE = 64.0
LOW = -1e30
ONES = 16
MOST_QUERIES = 1024
MOST_KEYS = 2048
LIMIT = 1e30
BF16 = jnp.bfloat16
F32 = jnp.float32
VMEM = pl.BlockSpec(memory_space=pltpu.VMEM)
NT = (((1,), (1,)), ((), ()))
TN = (((0,), (0,)), ((), ()))


MIB = 1024 * 1024


def params(mib=32):
    return pltpu.CompilerParams(vmem_limit_bytes=mib * MIB)


def lower_lanes(shape):
    return lax.broadcasted_iota(jnp.int32, shape, 1) < HEAD_DIM


def swap_halves(x):
    return pltpu.roll(x, HEAD_DIM, 1)


def pack_kernel(rest, per_group, q_hbm, k_hbm, v_hbm, valid_hbm, *refs):
    outs, (q_ref, k_ref, v_ref, valid_ref, sems) = refs[:GROUPS], refs[GROUPS:]
    copies = [
        pltpu.make_async_copy(src, dst, sems.at[i])
        for i, (src, dst) in enumerate(
            ((valid_hbm, valid_ref), (k_hbm, k_ref), (v_hbm, v_ref), (q_hbm, q_ref))
        )
    ]
    for copy in copies:
        copy.start()
    mine = lax.axis_index("inner") // rest
    rows = q_ref.shape[0]
    half = rows // 2
    for copy in copies:
        copy.wait()
    square = (rows, rows)
    on_diagonal = lax.broadcasted_iota(jnp.int32, square, 0) == lax.broadcasted_iota(
        jnp.int32, square, 1
    )
    flag_row = jnp.broadcast_to(valid_ref[...].astype(F32), square)
    picked = jnp.where(on_diagonal, flag_row, 0.0).astype(BF16)
    flags = jnp.dot(picked, jnp.ones((rows, LANES), BF16), preferred_element_type=F32) > 0.5
    low = lower_lanes((rows, LANES))
    low_half = lower_lanes((half, LANES))
    kv_groups, q_groups = [], []
    for g in range(GROUPS):
        kv_slots, q_slots = [], []
        for j in range(per_group):
            h = g * per_group + j
            tile = pl.ds((h // 2) * LANES, LANES)
            k = k_ref[:, tile].astype(F32)
            v = v_ref[:, tile].astype(F32)
            q = q_ref[:, tile].astype(F32) * (HEAD_DIM**-0.5)
            if h % 2 == 0:
                kv = jnp.where(low, k, swap_halves(v))
                qq = jnp.where(low_half, q[:half], swap_halves(q[half:]))
            else:
                kv = jnp.where(low, swap_halves(k), v)
                qq = jnp.where(low_half, swap_halves(q[:half]), q[half:])
            kv_slots.append(jnp.where(flags, kv, MARK))
            q_slots.append(qq)
        kv_groups.append(kv_slots)
        q_groups.append(q_slots)
    for s in range(GROUPS):
        want = jnp.bitwise_xor(mine, s)
        for j in range(per_group):
            lanes = pl.ds(j * LANES, LANES)
            for groups, start, n in ((kv_groups, 0, rows), (q_groups, rows, half)):
                x = groups[0][j]
                for g in range(1, GROUPS):
                    x = jnp.where(want == g, groups[g][j], x)
                outs[s][pl.ds(start, n), lanes] = x.astype(BF16)


def pack(q, k, v, valid, rest):
    rows, width = q.shape
    per_group = width // HEAD_DIM // GROUPS
    slots = per_group * LANES
    return pl.pallas_call(
        functools.partial(pack_kernel, rest, per_group),
        out_shape=[jax.ShapeDtypeStruct((rows + rows // 2, slots), BF16)] * GROUPS,
        in_specs=[pl.BlockSpec(memory_space=pltpu.HBM)] * 4,
        out_specs=[VMEM] * GROUPS,
        scratch_shapes=[pltpu.VMEM((rows, width), BF16)] * 3
        + [pltpu.VMEM((1, rows), jnp.int32), pltpu.SemaphoreType.DMA((4,))],
        compiler_params=params(24),
    )(*[pltpu.with_memory_space_constraint(x, pltpu.HBM) for x in (q, k, v, valid.reshape(1, rows))])


def spread_queries(refs, half, qs):
    start = 0
    for ref in refs:
        for piece in range(ref.shape[0] // half):
            for j in range(qs.shape[1] // LANES):
                lanes = pl.ds(j * LANES, LANES)
                x = ref[pl.ds(piece * half, half), lanes].astype(F32)
                low = lower_lanes(x.shape)
                qs[pl.ds(start, half), lanes] = jnp.where(low, x, 0.0).astype(BF16)
                qs[pl.ds(start + half, half), lanes] = jnp.where(low, swap_halves(x), 0.0).astype(BF16)
            start += 2 * half


def spread_keys(refs, ks, vs):
    start = 0
    for ref in refs:
        n = ref.shape[0]
        for j in range(ks.shape[1] // LANES):
            lanes = pl.ds(j * LANES, LANES)
            x = ref[:, lanes]
            hole = x > jnp.asarray(MARK_TEST, BF16)
            low = lower_lanes(x.shape)
            zero = jnp.zeros_like(x)
            x = jnp.where(hole, zero, x)
            ks[pl.ds(start, n), lanes] = x
            vs[pl.ds(start, n), lanes] = jnp.where(low, jnp.where(hole, zero, jnp.ones_like(x)), x)
        start += n


def largest_norm(ref):
    pick = lower_lanes((16, LANES)).astype(BF16)
    best = None
    for j in range(ref.shape[1] // LANES):
        x = ref[:, pl.ds(j * LANES, LANES)]
        norms = lax.dot_general(pick, x * x, NT, preferred_element_type=F32)
        best = norms if best is None else jnp.maximum(best, norms)
    return jnp.max(best[:8])


def add_keys(work, ks, vs, safe):
    slots = ks.shape[1] // LANES
    rows_k = ks.shape[0]
    steps = []
    for first_key, qs, old_acc, old_top, acc, top in work:
        top[...] = jnp.zeros_like(top) if old_top is None else old_top[...]
        for j in range(slots):
            for col in range(0, qs.shape[0], MOST_QUERIES):
                at = pl.ds(col, min(MOST_QUERIES, qs.shape[0] - col))
                for row in range(first_key, rows_k, MOST_KEYS):
                    ka = pl.ds(row, min(MOST_KEYS, rows_k - row))
                    steps.append((qs, old_acc if row == first_key else acc, acc, pl.ds(j * LANES, LANES), at, ka))

    def scores(step):
        qs, unused, unused, lanes, at, ka = step
        return lax.dot_general(ks[ka, lanes], qs[at, lanes], NT, preferred_element_type=F32)

    ahead = scores(steps[0])
    for i, (qs, base, acc, lanes, at, ka) in enumerate(steps):
        p = jnp.exp(ahead).astype(BF16)
        if i + 1 < len(steps):
            ahead = scores(steps[i + 1])
        term = lax.dot_general(vs[ka, lanes], p, TN, preferred_element_type=F32)
        acc[lanes, at] = term if base is None else base[lanes, at] + term

    @pl.when(jnp.logical_not(safe))
    def _():
        for first_key, qs, old_acc, unused, acc, top in work:
            acc[...] = jnp.zeros_like(acc) if old_acc is None else old_acc[...]
            add_keys_shifted(first_key, qs, ks, vs, acc, top)


def add_keys_shifted(first_key, qs, ks, vs, acc, top):
    slots = ks.shape[1] // LANES
    rows_k = ks.shape[0]
    cols = qs.shape[0]
    step_q, step_k = 128, 128

    def over_queries(i, unused):
        at = pl.ds(pl.multiple_of(i * step_q, step_q), step_q)
        for j in range(slots):
            lanes = pl.ds(j * LANES, LANES)

            def over_keys(c, carry):
                high, total = carry
                ka = pl.ds(pl.multiple_of(c * step_k, step_k), step_k)
                v = vs[ka, lanes]
                s = lax.dot_general(ks[ka, lanes], qs[at, lanes], NT, preferred_element_type=F32)
                s = jnp.where(v[:, :1].astype(F32) > 0.5, s, LOW)
                best = jnp.max(s, axis=0, keepdims=True)
                best = (best + jnp.abs(best) * (1.0 / 128)).astype(BF16).astype(F32)
                new = jnp.maximum(high, best)
                p = jnp.exp(s - new).astype(BF16)
                total = total * jnp.exp(high - new) + lax.dot_general(v, p, TN, preferred_element_type=F32)
                return new, total

            high, total = lax.fori_loop(first_key // step_k, rows_k // step_k, over_keys, (top[pl.ds(j, 1), at], acc[lanes, at]))
            acc[lanes, at] = total
            top[pl.ds(j, 1), at] = high
        return unused

    lax.fori_loop(0, cols // step_q, over_queries, 0)


def attend_kernel(sets, n_kv, half, first, n_export, *refs):
    given = []
    for n_q, unused in sets:
        count = n_q or 3
        given.append(refs[:count])
        refs = refs[count:]
    kv_refs, refs = refs[:n_kv], refs[n_kv:]
    if not first:
        info_in, refs = refs[0], refs[1:]
    held = []
    for (n_q, unused), mine in zip(sets, given):
        count = 3 if n_q else 2
        held.append(refs[:3] if n_q else (mine[0], *refs[:2]))
        refs = refs[count:]
    info, exports, (ks, vs) = refs[0], refs[1 : 1 + n_export], refs[1 + n_export :]
    length = None if first else info_in[...][0, 0]
    for (n_q, unused), mine, (qs, acc, top) in zip(sets, given, held):
        if n_q:
            spread_queries(mine, half, qs)
            own = largest_norm(qs)
            length = own if length is None else jnp.maximum(length, own)
    spread_keys(kv_refs, ks, vs)
    safe = jnp.logical_and(length * largest_norm(ks) * 1.05 <= SAFE * SAFE, length < LIMIT)
    info[...] = jnp.full(info.shape, jnp.where(safe, length, LIMIT), F32)
    work = []
    for (n_q, first_key), mine, (qs, acc, top) in zip(sets, given, held):
        old_acc, old_top = (None, None) if n_q else mine[1:]
        work.append((first_key, qs, old_acc, old_top, acc, top))
    add_keys(work, ks, vs, safe)
    for i, out in enumerate(exports):
        place = 0
        for qs, acc, top in held:
            cols = qs.shape[0] // (n_export + 1)
            at, to = pl.ds((i + 1) * cols, cols), pl.ds(place, cols)
            for j in range(qs.shape[1] // LANES):
                start = j * (HEAD_DIM + ONES)
                out[pl.ds(start, HEAD_DIM), to] = acc[pl.ds(j * LANES + HEAD_DIM, HEAD_DIM), at].astype(BF16)
                sums = acc[pl.ds(j * LANES, ONES), at]
                shift = jnp.broadcast_to(top[pl.ds(j, 1), at], sums.shape)
                upper = lax.broadcasted_iota(jnp.int32, sums.shape, 0) < ONES // 2
                out[pl.ds(start + HEAD_DIM, ONES), to] = jnp.where(upper, sums, shift).astype(BF16)
            place += cols


def attend(sets, kv_list, half, info, n_export=0):
    width = kv_list[0].shape[1]
    slots = width // LANES
    first = info is None
    rows_k = sum(k.shape[0] for k in kv_list)
    args, meta, out_shape, own_cols = [], [], [], 0
    for items, first_key in sets:
        new = items[0].dtype == items[1].dtype
        cols = sum(q.shape[0] for q in items) * 2 if new else items[0].shape[0]
        meta.append((len(items) if new else 0, first_key))
        if new:
            out_shape.append(jax.ShapeDtypeStruct((cols, width), BF16))
        out_shape += [jax.ShapeDtypeStruct((width, cols), F32), jax.ShapeDtypeStruct((8, cols), F32)]
        args += items
        own_cols += cols // (n_export + 1)
    args += kv_list
    if not first:
        args.append(info)
    out_shape.append(jax.ShapeDtypeStruct((8, LANES), F32))
    out_shape += [jax.ShapeDtypeStruct((slots * (HEAD_DIM + ONES), own_cols), BF16)] * n_export
    out = list(
        pl.pallas_call(
            functools.partial(attend_kernel, meta, len(kv_list), half, first, n_export),
            out_shape=out_shape,
            in_specs=[VMEM] * len(args),
            out_specs=[VMEM] * len(out_shape),
            scratch_shapes=[pltpu.VMEM((rows_k, width), BF16)] * 2,
            compiler_params=params(),
            cost_estimate=pl.CostEstimate(flops=1, bytes_accessed=1, transcendentals=0),
        )(*args)
    )
    states = []
    for (items, unused), (n_q, unused) in zip(sets, meta):
        states.append([out.pop(0) if n_q else items[0], out.pop(0), out.pop(0)])
    return states, out[0], out[1:]


def finish_kernel(n_sets, n_import, wanted, *refs):
    held = [refs[2 * i : 2 * i + 2] for i in range(n_sets)]
    imports, outs = refs[2 * n_sets : 2 * n_sets + n_import], list(refs[2 * n_sets + n_import :])
    piece = outs[0].shape[1]
    step = HEAD_DIM + ONES
    place = 0
    for acc, top in held:
        cols = acc.shape[1] // (n_import + 1)
        for col in range(0, cols, piece):
            if (place + col) // piece not in wanted:
                continue
            out = outs.pop(0)
            at, there = pl.ds(col, piece), pl.ds(place + col, piece)
            for j in range(acc.shape[0] // LANES):
                total = acc[pl.ds(j * LANES + HEAD_DIM, HEAD_DIM), at]
                count = acc[pl.ds(j * LANES, 1), at]
                high = top[pl.ds(j, 1), at]
                for ref in imports:
                    values = ref[pl.ds(j * step, HEAD_DIM), there].astype(F32)
                    both = ref[pl.ds(j * step + HEAD_DIM, ONES), there].astype(F32)
                    sums, shift = both[:1], both[ONES // 2 : ONES // 2 + 1]
                    new = jnp.maximum(high, shift)
                    mine, theirs = jnp.exp(high - new), jnp.exp(shift - new)
                    total = total * mine + values * theirs
                    count = count * mine + sums * theirs
                    high = new
                share = 1.0 / (count + jnp.exp(-high))
                out[pl.ds(j * HEAD_DIM, HEAD_DIM), :] = (total * share).astype(BF16)
        place += cols


def finish(states, imports, n_pieces, wanted):
    sums = [x for state in states for x in state[1:]]
    slots = sums[0].shape[0] // LANES
    piece = sum(state[1].shape[1] for state in states) // (len(imports) + 1) // n_pieces
    return pl.pallas_call(
        functools.partial(finish_kernel, len(states), len(imports), wanted),
        out_shape=[jax.ShapeDtypeStruct((slots * HEAD_DIM, piece), BF16)] * len(wanted),
        in_specs=[VMEM] * (len(sums) + len(imports)),
        out_specs=[VMEM] * len(wanted),
        compiler_params=params(),
    )(*sums, *imports)


def project_kernel(rest, *refs):
    parts, w_ref, out, joined = refs[:GROUPS], refs[GROUPS], refs[GROUPS + 1], refs[GROUPS + 2]
    mine = lax.axis_index("inner") // rest
    rows = parts[0].shape[0]
    for s, part in enumerate(parts):
        start = pl.multiple_of(jnp.bitwise_xor(mine, s) * rows, 16)
        joined[pl.ds(start, rows), :] = part[...]
    out[...] = lax.dot_general(joined[...], w_ref[...], TN, preferred_element_type=F32).astype(BF16)


def project(parts, w, rest):
    rows, cols = parts[0].shape
    return pl.pallas_call(
        functools.partial(project_kernel, rest),
        out_shape=jax.ShapeDtypeStruct((cols, w.shape[1]), BF16),
        in_specs=[VMEM] * (GROUPS + 1),
        out_specs=VMEM,
        scratch_shapes=[pltpu.VMEM((GROUPS * rows, cols), BF16)],
        compiler_params=params(),
    )(*parts, w)


def on_device(n_blk, n_inner, q, k, v, valid, w):
    rest = n_inner // GROUPS
    half = q.shape[0] // 2

    def over_groups(x, s):
        return lax.ppermute(x, "inner", [(i, (i // rest ^ s) * rest + i % rest) for i in range(n_inner)])

    def over_rest(x, t):
        return lax.ppermute(x, "inner", [(i, i // rest * rest + (i + t) % rest) for i in range(n_inner)])

    def over_blk(x, t):
        return lax.ppermute(x, "blk", [(i, (i + t) % n_blk) for i in range(n_blk)])

    def plane(chunk, order=(1, 2, 3)):
        return [lax.ppermute(chunk, "blk", [(b, b ^ d) for b in range(n_blk)]) for d in order]

    def after(x, *done):
        return lax.optimization_barrier((x, *done))[0]

    pieces = list(pack(q, k, v, valid, rest))
    rows = q.shape[0]

    def gathered_queries(pieces):
        own = jnp.concatenate([x[rows:] for x in pieces], axis=0)
        return [own] + [over_rest(own, t) for t in range(1, rest)]

    if n_blk == 4 and rest == 2:
        own0 = pieces[0][:rows]
        near0 = plane(own0, (3, 2, 1))
        pieces[2], pieces[1] = over_groups(pieces[2], 2), over_groups(pieces[1], 1)
        pieces[3] = over_groups(after(pieces[3], pieces[1], pieces[2]), 3)
        pieces[1], pieces[2] = after((pieces[1], pieces[2]), *near0)
        q_early = gathered_queries(pieces[:3])
        own1 = after(jnp.concatenate([x[:rows] for x in pieces[1:3]], axis=0), *q_early)
        near1 = plane(own1, (1, 2, 3))
        early = [own0, own1, *near0]
        (early_set,), info, unused = attend([(q_early, 0)], early, half, None)
        last = after(pieces[3], early_set[1])
        own2 = last[:rows]
        near2 = plane(own2, (3, 2, 1))
        q_late = gathered_queries([last])
        met = sum(x.shape[0] for x in early)
        states, info, unused = attend([(early_set, met), (q_late, 0)], [*early, own2], half, info)
        near1 = after(tuple(near1), states[0][1])
        states, info, unused = attend([(x, 0) for x in states], list(near1), half, info)
        states, info, exports = attend([(x, 0) for x in states], near2, half, info, rest - 1)
    else:
        pieces = [pieces[0]] + [over_groups(pieces[s], s) for s in range(1, GROUPS)]
        chunk = jnp.concatenate([x[:rows] for x in pieces], axis=0)
        blocks = [chunk] + [over_blk(chunk, t) for t in range(1, n_blk)]
        states, info, exports = attend([(gathered_queries(pieces), 0)], blocks, half, None, rest - 1)
    imports = [over_rest(x, rest - 1 - t) for t, x in enumerate(exports)]
    there = [over_groups(x, s) for s, x in zip((2, 3), finish(states, imports, GROUPS, (2, 3)))]
    own, beside = finish(states, imports, GROUPS, (0, 1))
    parts = [own, over_groups(beside, 1), *there]
    return project(parts, w, rest)


def solution(mesh):
    rows = P(("blk", "inner"), None)
    return jax.shard_map(
        functools.partial(on_device, mesh.shape["blk"], mesh.shape["inner"]),
        mesh=mesh,
        in_specs=(rows, rows, rows, P(("blk", "inner")), P()),
        out_specs=rows,
        check_vma=False,
    )
```
